32 devices in a mesh: req: 4 (over y, x), hid: 8 (over z, core).
Axes of the slice: x: 2, y: 2, z: 4, core: 2. Of those that a mesh axis runs over, the one named last changes fastest.
Arguments:
- tokens: bfloat16 [1024, 7168], P(('req', 'hid')), may hold values from -90 to 90
- gain_in: float32 [7168], replicated, may hold values from 0.25 to 1.75
- w_qkv: bfloat16 [7168, 3, 1792], P(None, None, 'hid'), may hold values from -0.0625 to 0.0625
- adapt_down: bfloat16 [7168, 128], replicated, may hold values from -0.0625 to 0.0625
- adapt_up: bfloat16 [128, 1792], P(None, 'hid'), may hold values from -0.5 to 0.5
- w_out: bfloat16 [1792, 3584], P('hid'), may hold values from -0.125 to 0.125
- gain_ff: float32 [3584], replicated, may hold values from 0.25 to 1.75
- w_gate_up: bfloat16 [3584, 2, 14336], P(None, None, 'hid'), may hold values from -0.09375 to 0.09375
- w_down: bfloat16 [14336, 3584], P('hid'), may hold values from -0.046875 to 0.046875
- prefix_cache: bfloat16 [4, 512, 2, 1792], P('req', 'hid'), may hold values from -330 to 330
- prefix_owner: int32 [3], replicated, may hold values from 0 to 3, as said below
- group_prefix: int32 [4], replicated, may hold values from 0 to 2, as said below
- lengths: int32 [4, 6], P('req'), may hold values from 1 to 128, 256 in all within a row
Outputs:
- attn_out: bfloat16 [1024, 3584], P(('req', 'hid'))
- block_out: bfloat16 [1024, 3584], P(('req', 'hid'))
The draws below stay inside these ranges and needn't reach their ends.
Inputs may be any that keep to these rules, and one draw needn't show every extreme that they name: `prefix_owner`: the 3 prefixes have different owners. `group_prefix`: every prefix is extended by at least one group. Each group's 6 lengths sum to 256, and the longest of each group is exactly 128.
All inputs are finite; a program needn't handle non-finite values.
Results may differ from the reference program's by a relative error of at most 0.035.
Values may be sent and summed in bfloat16 or wider, within the bound.
No kernel may reach another device: no remote copies, remote signals or barrier semaphores. Data moves between devices by JAX's collectives and lax.ppermute only.
A program may use at most 128 MiB of HBM per device.

```python
import math
import jax
import jax.numpy as jnp
import numpy as np
from jax import lax

DIN = 7168
DM = 3584
FF = 14336
HD = 224
RANK = 128
NPFX = 3
REQ_GRP = 6
HEADS = 8
DQ = 1792
PFX = 512
TOK_GRP = 256
TOKENS = 1024
N_REQ = 4


def draw_tokens(key, part):
    k_base, k_rows, k_cols = jax.random.split(key, 3)
    row_scale = jnp.exp(jax.random.uniform(k_rows, (TOKENS, 1), minval=math.log(0.3), maxval=math.log(3.0)))
    col_scale = jnp.exp(jax.random.uniform(k_cols, (1, DIN), minval=math.log(0.5), maxval=math.log(5.0)))
    base = jnp.clip(jax.random.normal(k_base, (TOKENS, DIN), dtype=jnp.float32), -6.0, 6.0)
    return (base * row_scale * col_scale).astype(jnp.bfloat16)


def draw_prefix_cache(key, part):
    k_base = jax.random.fold_in(key, 0)
    base = jnp.clip(jax.random.normal(k_base, (N_REQ, PFX, 2, DQ), dtype=jnp.float32), -6.0, 6.0)
    return base.astype(jnp.bfloat16)


def draw_prefix_owner(key, part):
    return jax.random.permutation(jax.random.fold_in(key, 7), N_REQ)[:NPFX].astype(jnp.int32)


def draw_group_prefix(key, part):
    k_first, k_rest, k_order = jax.random.split(jax.random.fold_in(key, 11), 3)
    first = jax.random.permutation(k_first, NPFX).astype(jnp.int32)
    rest = jax.random.randint(k_rest, (N_REQ - NPFX,), 0, NPFX).astype(jnp.int32)
    return jax.random.permutation(k_order, jnp.concatenate([first, rest])).astype(jnp.int32)


def block_scale(stream_key, dims, cuts, smallest, top_value):
    loudness = 1.0
    for axis_at, parts in cuts:
        steps = jax.random.uniform(jax.random.fold_in(jax.random.fold_in(stream_key, 6), axis_at), (parts,), jnp.float32, smallest / len(cuts), top_value / len(cuts))
        loudness = loudness * jnp.repeat(jnp.exp(steps), dims[axis_at] // parts).reshape((-1,) + (1,) * (len(dims) - 1 - axis_at))
    return loudness


def profile(count, total, most, lean):
    weights = [(1 << 20) // math.isqrt(rank ** lean) + 1 for rank in range(2, count + 1)]
    spare, holding = total - most - (count - 1), [1] * (count - 1)
    while spare > 0:
        candidates = [i for i in range(count - 1) if holding[i] < most]
        pool, remaining = sum([weights[i] for i in candidates]), spare
        for i in candidates:
            extra = min(most - holding[i], max(1, remaining * weights[i] // pool), spare)
            holding[i] = holding[i] + extra
            spare = spare - extra
    return np.array([most] + holding)


def ragged_sizes(key, number_of, total, most, lean):
    if number_of == 2:
        one = jax.random.randint(key, (), max(1, total - most), min(most, total - 1) + 1)
        return jnp.stack([one, total - one])
    tallies = jnp.asarray(profile(number_of, total, most, lean), jnp.int32)
    couples = (number_of - 1) // 2
    giver, sink = tallies[1:1 + 2 * couples:2], tallies[2:2 + 2 * couples:2]
    room = jnp.minimum(giver - 1, most - sink)
    passed = jax.random.randint(jax.random.fold_in(key, 1), (couples,), 0, 1 << 20) % (room + 1)
    tallies = tallies.at[1:1 + 2 * couples:2].set(giver - passed).at[2:2 + 2 * couples:2].set(sink + passed)
    return tallies[jax.random.permutation(jax.random.fold_in(key, 2), number_of)]


def scatter_about(key, extent, deviation, reach, cuts=(), kind=jnp.bfloat16):
    result = deviation * jax.random.normal(key, extent, jnp.float32)
    if cuts:
        result = result * block_scale(key, extent, cuts, -0.22, 0.18)
    return jnp.clip(result, -reach, reach).astype(kind)


def setup_inputs(seed: int = 0) -> dict:
    arg_keys = jax.random.split(jax.random.key(seed), 14)
    return {
        "tokens": draw_tokens(jax.random.fold_in(arg_keys[13], 71), 0),
        "gain_in": jnp.clip(1.0 + 0.15 * jax.random.normal(arg_keys[1], (DIN,), jnp.float32), 0.25, 1.75),
        "w_qkv": scatter_about(arg_keys[2], (DIN, 3, DQ), DIN ** -0.5, 0.0625, ((2, 8),)),
        "adapt_down": scatter_about(arg_keys[3], (DIN, RANK), DIN ** -0.5, 0.0625),
        "adapt_up": scatter_about(arg_keys[4], (RANK, DQ), RANK ** -0.5, 0.5, ((1, 8),)),
        "w_out": scatter_about(arg_keys[5], (DQ, DM), DQ ** -0.5, 0.125, ((0, 8),)),
        "gain_ff": jnp.clip(1.0 + 0.15 * jax.random.normal(arg_keys[6], (DM,), jnp.float32), 0.25, 1.75),
        "w_gate_up": scatter_about(arg_keys[7], (DM, 2, FF), DM ** -0.5, 0.09375, ((2, 8),)),
        "w_down": scatter_about(arg_keys[8], (FF, DM), FF ** -0.5, 0.046875, ((0, 8),)),
        "prefix_cache": draw_prefix_cache(jax.random.fold_in(arg_keys[13], 71), 0),
        "prefix_owner": draw_prefix_owner(jax.random.fold_in(arg_keys[13], 71), 0),
        "group_prefix": draw_group_prefix(jax.random.fold_in(arg_keys[13], 71), 0),
        "lengths": jax.vmap(lambda own: ragged_sizes(own, REQ_GRP, TOK_GRP, TOK_GRP // 2, 2))(jax.random.split(arg_keys[12], N_REQ)).reshape((N_REQ, REQ_GRP)).astype(jnp.int32),
    }


EPS = 1e-05

def rms_scale(matrix, gain_vec):
    return matrix * lax.rsqrt(lax.optimization_barrier(jnp.mean(matrix * matrix, axis=-1, keepdims=True)) + EPS) * gain_vec

def rounded_f32(matrix):
    return lax.optimization_barrier(matrix.astype(jnp.bfloat16)).astype(jnp.float32)

def reference(tokens, gain_in, w_qkv, adapt_down, adapt_up, w_out, gain_ff, w_gate_up, w_down, prefix_cache, prefix_owner, group_prefix, lengths):
    normed = rms_scale(tokens.astype(jnp.float32), gain_in).astype(jnp.bfloat16)
    latent = jnp.dot(normed, adapt_down, preferred_element_type=jnp.float32).astype(jnp.bfloat16)
    joint = jnp.dot(normed, w_qkv.reshape(DIN, 3 * DQ), preferred_element_type=jnp.float32)
    queries = (joint[:, :DQ] + jnp.dot(latent, adapt_up, preferred_element_type=jnp.float32)).astype(jnp.bfloat16)
    suffix_keys = joint[:, DQ:2 * DQ].astype(jnp.bfloat16)
    suffix_vals = joint[:, 2 * DQ:].astype(jnp.bfloat16)
    score_scale = HD ** (-0.5)
    position = jnp.arange(TOK_GRP, dtype=jnp.int32)
    outputs = []
    for group_index in range(N_REQ):
        row_begin = group_index * TOK_GRP
        group_q = queries[row_begin:row_begin + TOK_GRP].astype(jnp.float32).reshape(TOK_GRP, HEADS, HD)
        group_k = suffix_keys[row_begin:row_begin + TOK_GRP].astype(jnp.float32).reshape(TOK_GRP, HEADS, HD)
        group_v = suffix_vals[row_begin:row_begin + TOK_GRP].astype(jnp.float32).reshape(TOK_GRP, HEADS, HD)
        owner_slot = prefix_owner[group_prefix[group_index]]
        cached = prefix_cache[owner_slot].astype(jnp.float32)
        cached_k = cached[:, 0].reshape(PFX, HEADS, HD)
        cached_v = cached[:, 1].reshape(PFX, HEADS, HD)
        request_ends = jnp.cumsum(lengths[group_index]).astype(jnp.int32)
        request = lax.optimization_barrier(jnp.sum((position[:, None] >= request_ends[None, :]).astype(jnp.int32), axis=1))
        allowed = jnp.logical_and(request[:, None] == request[None, :], position[None, :] <= position[:, None])
        score_pre = jnp.einsum('thd,phd->htp', group_q, cached_k) * score_scale
        score_suf = jnp.einsum('thd,shd->hts', group_q, group_k) * score_scale
        score_suf = jnp.where(allowed[None], score_suf, -jnp.inf)
        row_max = jnp.maximum(lax.optimization_barrier(jnp.max(score_pre, axis=-1)), lax.optimization_barrier(jnp.max(score_suf, axis=-1)))
        expo_pre = jnp.exp(score_pre - row_max[..., None])
        expo_suf = jnp.exp(score_suf - row_max[..., None])
        row_sum = lax.optimization_barrier(jnp.sum(expo_pre, axis=-1)) + lax.optimization_barrier(jnp.sum(expo_suf, axis=-1))
        weighted = jnp.einsum('htp,phd->thd', rounded_f32(expo_pre), cached_v)
        weighted = weighted + jnp.einsum('hts,shd->thd', rounded_f32(expo_suf), group_v)
        heads_out = (weighted / row_sum.T[..., None]).astype(jnp.bfloat16).reshape(TOK_GRP, DQ)
        outputs.append(heads_out)
    heads_all = jnp.concatenate(outputs, axis=0)
    summed = jnp.dot(heads_all, w_out, preferred_element_type=jnp.float32)
    attn_out = summed.astype(jnp.bfloat16)
    ff_in = rms_scale(summed, gain_ff).astype(jnp.bfloat16)
    gate_up = jnp.dot(ff_in, w_gate_up.reshape(DM, 2 * FF), preferred_element_type=jnp.float32)
    hidden = (jax.nn.silu(gate_up[:, :FF]) * gate_up[:, FF:]).astype(jnp.bfloat16)
    block_out = jnp.dot(hidden, w_down, preferred_element_type=jnp.float32).astype(jnp.bfloat16)
    return (attn_out, block_out)
```

```python
import jax
import jax.numpy as jnp
from jax import lax
from jax.sharding import PartitionSpec as P

HD = 224
EPS = 1e-05
F32 = jnp.float32
BF16 = jnp.bfloat16


def ring_order(n):
    half = n // 2
    return [2 * q for q in range(half)] + [2 * (n - 1 - q) + 1 for q in range(half, n)]


def ring_steps(n):
    order = ring_order(n)
    fwd = [(order[i], order[(i + 1) % n]) for i in range(n)]
    bwd = [(order[i], order[(i - 1) % n]) for i in range(n)]
    return fwd, bwd


def split_cols(block, count):
    width = block.shape[1] // count
    return [block[:, i * width : (i + 1) * width] for i in range(count)]


def ring_gather(block, n, count):
    fwd, bwd = ring_steps(n)
    own = split_cols(block, count)
    slots = [None] * n
    slots[0] = own
    ahead, behind = list(own), list(own)
    for step in range(1, n // 2 + 1):
        ahead = [lax.ppermute(v, "hid", fwd) for v in ahead]
        slots[step] = list(ahead)
        if step < n // 2:
            behind = [lax.ppermute(v, "hid", bwd) for v in behind]
            slots[n - step] = list(behind)
    return jnp.concatenate([jnp.concatenate(s, axis=1) for s in slots], axis=0)


def ring_scatter(partial, n, count):
    fwd, bwd = ring_steps(n)
    rows = partial.shape[0] // n
    out = []
    for part in split_cols(partial, count):
        slot = lambda k: part[(k % n) * rows : (k % n + 1) * rows]
        ahead = slot(n // 2)
        for k in range(n // 2 + 1, n + 1):
            ahead = lax.ppermute(ahead.astype(BF16), "hid", fwd).astype(F32)
            if k < n:
                ahead = ahead + slot(k)
        behind = slot(n // 2 - 1)
        for k in range(n // 2 - 2, -1, -1):
            behind = lax.ppermute(behind.astype(BF16), "hid", bwd).astype(F32)
            if k > 0:
                behind = behind + slot(k)
        out.append(ahead + behind + slot(0))
    return jnp.concatenate(out, axis=1)


def rms_scale(matrix, gain_vec):
    return matrix * lax.rsqrt(jnp.mean(matrix * matrix, axis=-1, keepdims=True) + EPS) * gain_vec


def make(mesh):
    n = mesh.shape["hid"]
    n_req = mesh.shape["req"]
    half = n // 2

    def per_device(tokens, gain_in, w_qkv, adapt_down, adapt_up, w_out, gain_ff, w_gate_up, w_down,
                   prefix_cache, prefix_owner, group_prefix, lengths):
        tok_dev, width_in = tokens.shape
        cols = w_qkv.shape[2]
        model_width = w_out.shape[1]
        hid = lax.axis_index("hid")
        core = hid % 2
        chip = hid // 2
        place = jnp.where(core == 0, chip, n - 1 - chip)

        cache = prefix_cache[0].reshape(-1, 2, half, 2, cols)
        mine = lax.dynamic_index_in_dim(cache, core, 3, keepdims=False)
        other = lax.dynamic_index_in_dim(cache, 1 - core, 3, keepdims=False)
        both = [(h, h ^ 1) for h in range(n)]
        got = lax.ppermute(other, "hid", both)
        cache = jnp.concatenate([mine, got], axis=0)
        blocks = [lax.dynamic_index_in_dim(cache, chip, 2, keepdims=False)]
        for k in range(1, half):
            block = lax.dynamic_index_in_dim(cache, chip ^ k, 2, keepdims=False)
            blocks.append(lax.ppermute(block, "hid", [(h, h ^ (2 * k)) for h in range(n)]))
        heads_cache = jnp.concatenate(blocks, axis=0)

        normed = rms_scale(tokens.astype(F32), gain_in).astype(BF16)
        rows_in = ring_gather(normed, n, 2)

        req = lax.axis_index("req")
        target = prefix_owner[group_prefix[req]]
        away = target ^ req
        chosen = heads_cache
        for k in range(1, n_req):
            seen = lax.ppermute(heads_cache, "req", [(r, r ^ k) for r in range(n_req)])
            chosen = jnp.where(away == k, seen, chosen)

        latent = jnp.dot(rows_in, adapt_down, preferred_element_type=F32).astype(BF16)
        joint = jnp.dot(rows_in, w_qkv.reshape(width_in, 3 * cols), preferred_element_type=F32)
        queries = (joint[:, :cols] + jnp.dot(latent, adapt_up, preferred_element_type=F32)).astype(BF16)
        keys = joint[:, cols : 2 * cols].astype(BF16)
        vals = joint[:, 2 * cols :].astype(BF16)
        tok_grp = rows_in.shape[0]
        spot = (place - jnp.arange(n, dtype=jnp.int32)) % n
        owner = jnp.where(spot < half, 2 * spot, 2 * (n - 1 - spot) + 1)
        position = (owner[:, None] * tok_dev + jnp.arange(tok_dev, dtype=jnp.int32)[None, :]).reshape(-1)
        ends = jnp.cumsum(lengths[0])
        request = jnp.sum((position[:, None] >= ends[None, :]).astype(jnp.int32), axis=1)
        allowed = jnp.logical_and(request[:, None] == request[None, :], position[None, :] <= position[:, None])
        nt = (((1,), (1,)), ((), ()))
        scale = HD ** (-0.5)
        pre = lax.dot_general(queries, chosen[:, 0], nt, preferred_element_type=F32) * scale
        suf = lax.dot_general(queries, keys, nt, preferred_element_type=F32) * scale
        suf = jnp.where(allowed, suf, -jnp.inf)
        top = jnp.maximum(jnp.max(pre, axis=1), jnp.max(suf, axis=1))[:, None]
        pre = jnp.exp(pre - top)
        suf = jnp.exp(suf - top)
        total = jnp.sum(pre, axis=1) + jnp.sum(suf, axis=1)
        weighted = jnp.dot(pre.astype(BF16), chosen[:, 1], preferred_element_type=F32) + jnp.dot(
            suf.astype(BF16), vals, preferred_element_type=F32
        )
        heads_out = (weighted / total[:, None]).astype(BF16)
        partial = jnp.dot(heads_out, w_out, preferred_element_type=F32)
        attn_own = ring_scatter(partial, n, 2).astype(BF16)
        summed = ring_gather(attn_own, n, 2).astype(F32)

        ff_in = rms_scale(summed, gain_ff).astype(BF16)
        units = w_gate_up.shape[2]
        gate_up = jnp.dot(ff_in, w_gate_up.reshape(model_width, 2 * units), preferred_element_type=F32)
        hidden = (jax.nn.silu(gate_up[:, :units]) * gate_up[:, units:]).astype(BF16)
        down = jnp.dot(hidden, w_down, preferred_element_type=F32)
        block_own = ring_scatter(down, n, 2).astype(BF16)
        return attn_own, block_own

    return per_device


def solution(mesh):
    placed = (
        P(("req", "hid"), None),
        P(),
        P(None, None, "hid"),
        P(),
        P(None, "hid"),
        P("hid", None),
        P(),
        P(None, None, "hid"),
        P("hid", None),
        P("req", "hid", None, None),
        P(),
        P(),
        P("req", None),
    )
    return jax.shard_map(
        make(mesh),
        mesh=mesh,
        in_specs=placed,
        out_specs=(P(("req", "hid"), None), P(("req", "hid"), None)),
        check_vma=False,
    )
```

```python
import functools

import jax
import jax.numpy as jnp
from jax import lax
from jax.experimental import pallas as pl
from jax.experimental.pallas import tpu as pltpu
from jax.sharding import PartitionSpec as P

HD = 224
EPS = 1e-05
F32 = jnp.float32
BF16 = jnp.bfloat16
NT = (((1,), (1,)), ((), ()))
VMEM = pl.BlockSpec(memory_space=pltpu.VMEM)
SMEM = pl.BlockSpec(memory_space=pltpu.SMEM)
ANY = pl.BlockSpec(memory_space=pl.ANY)


def params(mib=56):
    return pltpu.CompilerParams(vmem_limit_bytes=mib * 2**20)


def split_cols(block, count):
    width = block.shape[1] // count
    return [block[:, i * width : (i + 1) * width] for i in range(count)]


def tile_of(width):
    return 256 if width % 256 == 0 else width


def norm_body(tok_ref, gain_ref, *outs):
    t = tok_ref[...].astype(F32)
    scale = lax.rsqrt(jnp.mean(t * t, axis=-1, keepdims=True) + EPS)
    normed = (t * scale * gain_ref[...]).astype(BF16)
    width = t.shape[1] // len(outs)
    for i, out in enumerate(outs):
        out[...] = normed[:, i * width : (i + 1) * width]


def norm_rows(tokens, gain, count):
    rows, width = tokens.shape
    return pl.pallas_call(
        norm_body,
        in_specs=[VMEM, VMEM],
        out_specs=[VMEM] * count,
        out_shape=[jax.ShapeDtypeStruct((rows, width // count), BF16)] * count,
        compiler_params=params(16),
        name="norm_rows",
    )(tokens, gain)


def unpair_body(w_ref, _, out_ref):
    out_ref[...] = jnp.swapaxes(w_ref[...], 0, 1)


def unpair(weights, part, parts, after):
    depth, two, width = weights.shape
    rows = depth // parts
    step = rows // 2
    return pl.pallas_call(
        unpair_body,
        grid=(2,),
        in_specs=[pl.BlockSpec((step, two, width), lambda i: (2 * part + i, 0, 0)), ANY],
        out_specs=pl.BlockSpec((two, step, width), lambda i: (0, i, 0)),
        out_shape=jax.ShapeDtypeStruct((two, rows, width), BF16),
        compiler_params=params(40),
        cost_estimate=pl.CostEstimate(flops=0, bytes_accessed=4 * rows * two * width, transcendentals=0),
        name="unpair",
    )(weights, after)


def project_step(pieces, w_ref, down_ref, rows_ref, acc_ref, lat_ref, first):
    step = pl.program_id(0)
    kb = w_ref.shape[1]

    @pl.when(step == 0)
    def _():
        at = 0
        for piece in pieces:
            n = piece.shape[0]
            for s in range(rows_ref.shape[0]):
                rows_ref[s, at : at + n, :] = piece[:, s * kb : (s + 1) * kb]
            at += n
        first()

    x = rows_ref[step]
    acc_ref[...] += lax.dot_general(x, w_ref[...], NT, preferred_element_type=F32)
    lat_ref[...] += jnp.dot(x, down_ref[...], preferred_element_type=F32)


def project_body(count, *refs):
    pieces, (w_ref, down_ref, acc_ref, lat_ref, rows_ref) = refs[:count], refs[count:]

    def first():
        acc_ref[...] = jnp.zeros_like(acc_ref)
        lat_ref[...] = jnp.zeros_like(lat_ref)

    project_step(pieces, w_ref, down_ref, rows_ref, acc_ref, lat_ref, first)


def attend_body(count, dims, place_ref, len_ref, *refs):
    pieces = refs[:count]
    w_ref, down_ref, up_ref, kv_ref, acc_in, lat_in, out_ref, rows_ref, acc_ref, lat_ref = refs[count:]
    rows, cols, chips, tok_dev = dims
    steps = rows_ref.shape[0]

    def first():
        acc_ref[...] = acc_in[...]
        lat_ref[...] = lat_in[...]

    project_step(pieces, w_ref, down_ref, rows_ref, acc_ref, lat_ref, first)

    @pl.when(pl.program_id(0) == steps - 1)
    def _():
        chip, core = place_ref[0], place_ref[1]
        keys = acc_ref[:, cols : 2 * cols].astype(BF16)
        vals = acc_ref[:, 2 * cols :].astype(BF16)
        up = up_ref[...]
        scale = HD ** (-0.5)
        pair = 2 * tok_dev

        def spots(row):
            slot = row // pair
            inside = row - slot * pair
            side = inside // tok_dev
            owner = chip - slot
            owner = jnp.where(owner < 0, owner + chips, owner)
            at = jnp.where(core == 0, side, 1 - side)
            return owner * pair + at * tok_dev + inside - side * tok_dev

        def requests(spot):
            end = len_ref[0, 0]
            found = (spot >= end).astype(jnp.int32)
            for j in range(1, len_ref.shape[1]):
                end = end + len_ref[0, j]
                found = found + (spot >= end).astype(jnp.int32)
            return found

        block = min(256, rows)
        col_spot = spots(lax.broadcasted_iota(jnp.int32, (1, rows), 1))
        col_req = requests(col_spot)

        def one_block(b, carry):
            r0 = pl.multiple_of(b * block, block)
            lat = lat_ref[pl.ds(r0, block), :].astype(BF16)
            q = acc_ref[pl.ds(r0, block), :cols] + lax.dot_general(lat, up, NT, preferred_element_type=F32)
            q = q.astype(BF16)
            row_spot = spots(r0 + lax.broadcasted_iota(jnp.int32, (block, 1), 0))
            allowed = jnp.logical_and(requests(row_spot) == col_req, col_spot <= row_spot)
            pre = lax.dot_general(q, kv_ref[0], NT, preferred_element_type=F32) * scale
            suf = lax.dot_general(q, keys, NT, preferred_element_type=F32) * scale
            suf = jnp.where(allowed, suf, -jnp.inf)
            top = jnp.maximum(jnp.max(pre, axis=1, keepdims=True), jnp.max(suf, axis=1, keepdims=True))
            pre = jnp.exp(pre - top)
            suf = jnp.exp(suf - top)
            total = jnp.sum(pre, axis=1, keepdims=True) + jnp.sum(suf, axis=1, keepdims=True)
            weighted = jnp.dot(pre.astype(BF16), kv_ref[1], preferred_element_type=F32) + jnp.dot(
                suf.astype(BF16), vals, preferred_element_type=F32
            )
            heads = (weighted / total).astype(BF16)
            for k in range(block // tok_dev):
                base = r0 + (k // 2) * pair
                shift = (core if k % 2 == 0 else 1 - core) * tok_dev
                at = pl.multiple_of(base + shift, tok_dev)
                out_ref[pl.ds(at, tok_dev), :] = heads[k * tok_dev : (k + 1) * tok_dev]
            return carry

        if rows == block:
            one_block(0, 0)
        else:
            lax.fori_loop(0, rows // block, one_block, 0)


def project_specs(part, cols3, rank, width):
    kb = width // 4
    return 4, kb, [
        pl.BlockSpec((cols3, kb), lambda i: (0, 4 * part + i)),
        pl.BlockSpec((kb, rank), lambda i: (4 * part + i, 0)),
    ]


def project(pieces, part, w_t, down):
    rows = sum(p.shape[0] for p in pieces)
    width = pieces[0].shape[1]
    cols3, rank = w_t.shape[0], down.shape[1]
    steps, kb, specs = project_specs(part, cols3, rank, width)
    whole = lambda shape: pl.BlockSpec(shape, lambda i: (0, 0))
    return pl.pallas_call(
        functools.partial(project_body, len(pieces)),
        grid=(steps,),
        in_specs=[VMEM] * len(pieces) + specs,
        out_specs=[whole((rows, cols3)), whole((rows, rank))],
        out_shape=[jax.ShapeDtypeStruct((rows, cols3), F32), jax.ShapeDtypeStruct((rows, rank), F32)],
        scratch_shapes=[pltpu.VMEM((steps, rows, kb), BF16)],
        compiler_params=params(),
        cost_estimate=pl.CostEstimate(
            flops=2 * rows * width * (cols3 + rank), bytes_accessed=2 * width * (cols3 + rank), transcendentals=0
        ),
        name="project",
    )(*pieces, w_t, down)


def attend(pieces, part, w_t, down, up_t, kv, acc, lat, place, lengths, chips):
    rows = sum(p.shape[0] for p in pieces)
    width = pieces[0].shape[1]
    cols3, rank = w_t.shape[0], down.shape[1]
    cols = cols3 // 3
    steps, kb, specs = project_specs(part, cols3, rank, width)
    dims = (rows, cols, chips, pieces[0].shape[0])
    return pl.pallas_call(
        functools.partial(attend_body, len(pieces), dims),
        grid=(steps,),
        in_specs=[SMEM, SMEM] + [VMEM] * len(pieces) + specs + [VMEM] * 4,
        out_specs=pl.BlockSpec((rows, cols), lambda i: (0, 0)),
        out_shape=jax.ShapeDtypeStruct((rows, cols), BF16),
        scratch_shapes=[
            pltpu.VMEM((steps, rows, kb), BF16),
            pltpu.VMEM((rows, cols3), F32),
            pltpu.VMEM((rows, rank), F32),
        ],
        compiler_params=params(),
        cost_estimate=pl.CostEstimate(
            flops=2 * rows * width * (cols3 + rank), bytes_accessed=2 * width * (cols3 + rank), transcendentals=0
        ),
        name="attend",
    )(place, lengths, *pieces, w_t, down, up_t, kv, acc, lat)


def out_body(a_ref, b_ref, wa_ref, wb_ref, out_ref):
    out_ref[...] = jnp.dot(a_ref[...], wa_ref[...], preferred_element_type=F32) + jnp.dot(
        b_ref[...], wb_ref[...], preferred_element_type=F32
    )


def out_project(own, got, w_own, w_got):
    rows, cols = own.shape
    width = w_own.shape[1]
    tile = 896 if width % 896 == 0 else width
    whole = pl.BlockSpec((rows, cols), lambda j: (0, 0))
    wide = pl.BlockSpec((cols, tile), lambda j: (0, j))
    return pl.pallas_call(
        out_body,
        grid=(width // tile,),
        in_specs=[whole, whole, wide, wide],
        out_specs=pl.BlockSpec((rows, tile), lambda j: (0, j)),
        out_shape=jax.ShapeDtypeStruct((rows, width), F32),
        compiler_params=params(),
        name="out_project",
    )(own, got, w_own, w_got)


def gate_body(count, dims, place_ref, gain_ref, *refs):
    slots, chunks, parts = dims
    pieces = refs[:count]
    weights = refs[count : count + parts]
    out_ref, x_ref = refs[count + parts :]
    core = place_ref[1]
    half = x_ref.shape[2]

    @pl.when(pl.program_id(0) == 0)
    def _():
        at = iter(pieces)
        row = 0
        for _k in range(slots):
            own = [next(at)[...].astype(F32) for _c in range(chunks)]
            got = [next(at)[...].astype(F32) for _c in range(chunks)]
            own = jnp.concatenate(own, axis=1)
            got = jnp.concatenate(got, axis=1)
            n = own.shape[0]
            square = jnp.sum(own * own, axis=-1, keepdims=True) + jnp.sum(got * got, axis=-1, keepdims=True)
            scale = lax.rsqrt(square * (0.5 / half) + EPS)
            x_ref[core, row : row + n, :] = (own * scale * gain_ref[core]).astype(BF16)
            x_ref[1 - core, row : row + n, :] = (got * scale * gain_ref[1 - core]).astype(BF16)
            row += n

    gate = up = None
    per = half * 2 // parts
    for p, w_ref in enumerate(weights):
        side, at = divmod(p * per, half)
        x = x_ref[side, :, at : at + per]
        g = jnp.dot(x, w_ref[0], preferred_element_type=F32)
        u = jnp.dot(x, w_ref[1], preferred_element_type=F32)
        gate = g if gate is None else gate + g
        up = u if up is None else up + u
    out_ref[...] = (gate / (1.0 + jnp.exp(-gate)) * up).astype(BF16)


def gate_up(pieces, slots, chunks, weights, gain, place):
    half = gain.shape[2]
    rows = slots * pieces[0].shape[0]
    parts = len(weights)
    _, depth, units = weights[0].shape
    tile = tile_of(units)
    return pl.pallas_call(
        functools.partial(gate_body, len(pieces), (slots, chunks, parts)),
        grid=(units // tile,),
        in_specs=[SMEM, VMEM] + [VMEM] * len(pieces) + [pl.BlockSpec((2, depth, tile), lambda j: (0, 0, j))] * parts,
        out_specs=pl.BlockSpec((rows, tile), lambda j: (0, j)),
        out_shape=jax.ShapeDtypeStruct((rows, units), BF16),
        scratch_shapes=[pltpu.VMEM((2, rows, half), BF16)],
        compiler_params=params(),
        cost_estimate=pl.CostEstimate(
            flops=8 * rows * half * units, bytes_accessed=8 * half * units, transcendentals=rows * units
        ),
        name="gate_up",
    )(place, gain, *pieces, *weights)


def down_body(side_ref, x_ref, w_ref, *rest):
    out_ref = rest[-1]
    total = jnp.dot(x_ref[...], w_ref[...], preferred_element_type=F32)
    out_ref[...] = total.astype(out_ref.dtype)


def down_half(hidden, w_down, side, dtype):
    rows, units = hidden.shape
    half = w_down.shape[1] // 2
    tile = tile_of(half)
    steps = half // tile
    return pl.pallas_call(
        down_body,
        grid_spec=pltpu.PrefetchScalarGridSpec(
            num_scalar_prefetch=1,
            grid=(steps,),
            in_specs=[
                pl.BlockSpec((rows, units), lambda j, s: (0, 0)),
                pl.BlockSpec((units, tile), lambda j, s: (0, s[0] * steps + j)),
            ],
            out_specs=pl.BlockSpec((rows, tile), lambda j, s: (0, j)),
        ),
        out_shape=jax.ShapeDtypeStruct((rows, half), dtype),
        compiler_params=params(),
        cost_estimate=pl.CostEstimate(
            flops=2 * rows * half * units, bytes_accessed=2 * half * units, transcendentals=0
        ),
        name="down_half",
    )(side, hidden, w_down)


def make(mesh):
    n = mesh.shape["hid"]
    n_req = mesh.shape["req"]
    chips = n // 2
    both = [(h, h ^ 1) for h in range(n)]
    ring = [(h, (h + 2) % n) for h in range(n)]

    def swap(v):
        return lax.ppermute(v, "hid", both)

    def onward(v):
        return lax.ppermute(v, "hid", ring)

    def gather(own):
        slots = []
        here = list(own)
        for k in range(chips):
            if k:
                here = [onward(v) for v in here]
            slots.append(here)
        return [(s, [swap(v) for v in s]) for s in slots]

    def scatter(partial, count):
        rows = partial.shape[0] // chips
        parts = split_cols(partial, count)
        block = lambda i, k: parts[i][k * rows : (k + 1) * rows]
        sums = [block(i, 1).astype(BF16) for i in range(count)]
        for k in range(2, chips + 1):
            sums = [onward(v) for v in sums]
            sums = [v.astype(F32) + block(i, k % chips) for i, v in enumerate(sums)]
            sums = [v.astype(BF16) for v in sums]
        return sums

    def per_device(tokens, gain_in, w_qkv, adapt_down, adapt_up, w_out, gain_ff, w_gate_up, w_down,
                   prefix_cache, prefix_owner, group_prefix, lengths):
        tok_dev, width_in = tokens.shape
        cols = w_qkv.shape[2]
        model_width = w_out.shape[1]
        half = model_width // 2
        hid = lax.axis_index("hid")
        core = hid % 2
        chip = hid // 2
        place = jnp.stack([chip, core]).astype(jnp.int32)

        normed = norm_rows(tokens, gain_in[None, :], 2)
        slots = gather(normed)

        cache = jnp.swapaxes(prefix_cache[0], 0, 1).reshape(2, -1, chips, 2, cols)
        mine = lax.dynamic_index_in_dim(cache, core, 3, keepdims=False)
        other = lax.dynamic_index_in_dim(cache, 1 - core, 3, keepdims=False)
        cache = jnp.concatenate([mine, swap(other)], axis=1)
        blocks = [lax.dynamic_index_in_dim(cache, chip, 2, keepdims=False)]
        for k in range(1, chips):
            block = lax.dynamic_index_in_dim(cache, chip ^ k, 2, keepdims=False)
            blocks.append(lax.ppermute(block, "hid", [(h, h ^ (2 * k)) for h in range(n)]))
        heads_cache = jnp.concatenate(blocks, axis=1)
        req = lax.axis_index("req")
        away = prefix_owner[group_prefix[req]] ^ req
        chosen = heads_cache
        for k in range(1, n_req):
            seen = lax.ppermute(heads_cache, "req", [(r, r ^ k) for r in range(n_req)])
            chosen = jnp.where(away == k, seen, chosen)

        w_own = lax.dynamic_slice_in_dim(w_out, core * half, half, 1)
        w_got = swap(lax.dynamic_slice_in_dim(w_out, (1 - core) * half, half, 1))

        parts = 4
        w_pairs = [unpair(w_gate_up, p, parts, slots[min(p, chips - 1)][0][0]) for p in range(parts)]

        w_t = jnp.transpose(w_qkv, (1, 2, 0)).reshape(3 * cols, width_in)
        pick = lambda i: [v for s in slots for v in (s[0][i], s[1][i])]
        acc, lat = project(pick(0), 0, w_t, adapt_down)
        heads = attend(pick(1), 1, w_t, adapt_down, adapt_up.T, chosen, acc, lat, place, lengths, chips)
        partial = out_project(heads, swap(heads), w_own, w_got)

        sums = scatter(partial, 2)
        summed = gather(sums)
        own_rows = lambda v: lax.dynamic_slice_in_dim(v, core * tok_dev, tok_dev, 0)
        near = jnp.concatenate([own_rows(v) for v in summed[0][0]], axis=1)
        far = jnp.concatenate([own_rows(v) for v in summed[0][1]], axis=1)
        attn_own = jnp.where(core == 0, jnp.concatenate([near, far], axis=1), jnp.concatenate([far, near], axis=1))

        pieces = [v for s in summed for v in s[0] + s[1]]
        hidden = gate_up(pieces, chips, 2, w_pairs, gain_ff.reshape(2, 1, half), place)
        away_half = down_half(hidden, w_down, (1 - core).astype(jnp.int32)[None], BF16)
        got_half = swap(away_half)
        own_half = down_half(hidden, w_down, core.astype(jnp.int32)[None], F32)
        ends = scatter(own_half + got_half.astype(F32), 2)
        ends = jnp.concatenate(ends, axis=1)
        near = own_rows(ends)
        far = swap(lax.dynamic_slice_in_dim(ends, (1 - core) * tok_dev, tok_dev, 0))
        block_own = jnp.where(core == 0, jnp.concatenate([near, far], axis=1), jnp.concatenate([far, near], axis=1))
        return attn_own, block_own

    return per_device


def solution(mesh):
    placed = (
        P(("req", "hid"), None),
        P(),
        P(None, None, "hid"),
        P(),
        P(None, "hid"),
        P("hid", None),
        P(),
        P(None, None, "hid"),
        P("hid", None),
        P("req", "hid", None, None),
        P(),
        P(),
        P("req", None),
    )
    return jax.shard_map(
        make(mesh),
        mesh=mesh,
        in_specs=placed,
        out_specs=(P(("req", "hid"), None), P(("req", "hid"), None)),
        check_vma=False,
    )
```

```python
import functools

import jax
import jax.numpy as jnp
from jax import lax
from jax.experimental import pallas as pl
from jax.experimental.pallas import tpu as pltpu
from jax.sharding import PartitionSpec as P

HD = 224
EPS = 1e-05
F32 = jnp.float32
BF16 = jnp.bfloat16
NT = (((1,), (1,)), ((), ()))
TN = (((0,), (0,)), ((), ()))
VMEM = pl.BlockSpec(memory_space=pltpu.VMEM)
SMEM = pl.BlockSpec(memory_space=pltpu.SMEM)
ANY = pl.BlockSpec(memory_space=pl.ANY)
TOKEN = jax.ShapeDtypeStruct((8, 128), F32)
QUICK = pl.CostEstimate(flops=1, bytes_accessed=1, transcendentals=0)
HBM = pl.BlockSpec(memory_space=pltpu.HBM)


def params(mib=56):
    return pltpu.CompilerParams(vmem_limit_bytes=mib * 2**20)


def split_cols(block, count):
    width = block.shape[1] // count
    return [block[:, i * width : (i + 1) * width] for i in range(count)]


def tile_of(width):
    return 256 if width % 256 == 0 else width


def norm_body(tok_ref, gain_ref, *outs):
    t = tok_ref[...].astype(F32)
    scale = lax.rsqrt(jnp.mean(t * t, axis=-1, keepdims=True) + EPS)
    normed = (t * scale * gain_ref[...]).astype(BF16)
    width = t.shape[1] // len(outs)
    for i, out in enumerate(outs):
        out[...] = normed[:, i * width : (i + 1) * width]


def norm_rows(tokens, gain, count):
    rows, width = tokens.shape
    return pl.pallas_call(
        norm_body,
        in_specs=[VMEM, VMEM],
        out_specs=[VMEM] * count,
        out_shape=[jax.ShapeDtypeStruct((rows, width // count), BF16)] * count,
        compiler_params=params(16),
        cost_estimate=QUICK,
        name="norm_rows",
    )(tokens, gain)


def unpair_body(first, w_ref, _, out_ref, token_ref, buf, sems):
    token_ref[...] = jnp.zeros_like(token_ref)
    count, step = buf.shape[:2]

    def fetch(i):
        return pltpu.make_async_copy(w_ref.at[pl.ds(first + i * step, step)], buf.at[i], sems.at[i])

    for i in range(count):
        fetch(i).start()
    for i in range(count):
        fetch(i).wait()
        out_ref[:, i * step : (i + 1) * step, :] = jnp.swapaxes(buf[i], 0, 1)


def unpair(weights, part, parts, after):
    depth, two, width = weights.shape
    rows = depth // parts
    count = 4
    step = rows // count
    return pl.pallas_call(
        functools.partial(unpair_body, part * rows),
        in_specs=[HBM, ANY],
        out_specs=[VMEM] * 2,
        out_shape=[jax.ShapeDtypeStruct((two, rows, width), BF16), TOKEN],
        scratch_shapes=[pltpu.VMEM((count, step, two, width), BF16), pltpu.SemaphoreType.DMA((count,))],
        compiler_params=params(10),
        cost_estimate=QUICK,
        name="unpair",
    )(pltpu.with_memory_space_constraint(weights, pltpu.HBM), after)


def hold_body(place_ref, w_ref, down_ref, _, w_out, down_out, token_ref, sems):
    token_ref[...] = jnp.zeros_like(token_ref)
    copies = [pltpu.make_async_copy(down_ref, down_out, sems.at[0])]
    count = sems.shape[0] - 1
    step = w_ref.shape[0] // count
    for i in range(count):
        rows = pl.ds(i * step, step)
        copies.append(pltpu.make_async_copy(w_ref.at[rows], w_out.at[rows], sems.at[1 + i]))
    for c in copies:
        c.start()
    for c in copies:
        c.wait()


def hold(w_t, down, place, after):
    return pl.pallas_call(
        hold_body,
        in_specs=[SMEM, HBM, HBM, ANY],
        out_specs=[VMEM] * 3,
        out_shape=[jax.ShapeDtypeStruct(w_t.shape, BF16), jax.ShapeDtypeStruct(down.shape, BF16), TOKEN],
        scratch_shapes=[pltpu.SemaphoreType.DMA((7,))],
        compiler_params=params(2),
        cost_estimate=QUICK,
        name="hold",
    )(place, pltpu.with_memory_space_constraint(w_t, pltpu.HBM), pltpu.with_memory_space_constraint(down, pltpu.HBM), after)


def bring_body(flip, place_ref, w_ref, _, out_ref, token_ref, sems):
    token_ref[...] = jnp.zeros_like(token_ref)
    units, half = out_ref.shape
    core = place_ref[1]
    at = pl.multiple_of((1 - core if flip else core) * half, 128)
    count = sems.shape[0]
    step = units // count

    def fetch(i):
        rows = pl.ds(i * step, step)
        return pltpu.make_async_copy(w_ref.at[rows, pl.ds(at, half)], out_ref.at[rows], sems.at[i])

    for i in range(count):
        fetch(i).start()
    for i in range(count):
        fetch(i).wait()


def bring(w_down, place, flip, after):
    units, width = w_down.shape
    return pl.pallas_call(
        functools.partial(bring_body, flip),
        in_specs=[SMEM, HBM, ANY],
        out_specs=[VMEM] * 2,
        out_shape=[jax.ShapeDtypeStruct((units, width // 2), BF16), TOKEN],
        scratch_shapes=[pltpu.SemaphoreType.DMA((4,))],
        compiler_params=params(2),
        cost_estimate=QUICK,
        name="bring",
    )(place, pltpu.with_memory_space_constraint(w_down, pltpu.HBM), after)


def pass_body(_in, _token, _out):
    pass


def pass_on(value, token):
    return pl.pallas_call(
        pass_body,
        in_specs=[ANY, ANY],
        out_specs=ANY,
        out_shape=jax.ShapeDtypeStruct(value.shape, value.dtype),
        input_output_aliases={0: 0},
        compiler_params=params(1),
        cost_estimate=QUICK,
        name="pass_on",
    )(value, token)


def split_body(count, place_ref, owner_ref, group_ref, *refs):
    candidates = refs[:count]
    mine_ref, other_ref = refs[-2:]
    core, req = place_ref[1], place_ref[2]
    away = owner_ref[group_ref[req]] ^ req
    chips = mine_ref.shape[0]
    cols = mine_ref.shape[3]
    chosen = candidates[0][...]
    for k in range(1, count):
        chosen = jnp.where(away == k, candidates[k][...], chosen)
    chosen = jnp.swapaxes(chosen, 0, 1)
    for c in range(chips):
        even = chosen[:, :, 2 * c * cols : (2 * c + 1) * cols]
        odd = chosen[:, :, (2 * c + 1) * cols : (2 * c + 2) * cols]
        mine_ref[c] = jnp.where(core == 0, even, odd)
        other_ref[c] = jnp.where(core == 0, odd, even)


def split_heads(candidates, place, owner, group, chips, ties):
    positions, two, width = candidates[0].shape
    shape = jax.ShapeDtypeStruct((chips, two, positions, width // (2 * chips)), BF16)
    return pl.pallas_call(
        functools.partial(split_body, len(candidates)),
        in_specs=[SMEM] * 3 + [VMEM] * len(candidates) + [ANY] * len(ties),
        out_specs=[VMEM] * 2,
        out_shape=[shape] * 2,
        compiler_params=params(16),
        cost_estimate=QUICK,
        name="split_heads",
    )(place, owner, group, *candidates, *ties)


def pack_body(place_ref, mine_ref, got_ref, *outs):
    chip = place_ref[0]
    for k, out in enumerate(outs):
        out[0] = mine_ref[chip ^ k]
        out[1] = got_ref[chip ^ k]


def pack_blocks(mine, got, place):
    chips = mine.shape[0]
    shape = jax.ShapeDtypeStruct((2, *mine.shape[1:]), BF16)
    return pl.pallas_call(
        pack_body,
        in_specs=[SMEM, VMEM, VMEM],
        out_specs=[VMEM] * chips,
        out_shape=[shape] * chips,
        compiler_params=params(4),
        cost_estimate=QUICK,
        name="pack_blocks",
    )(place, mine, got)


def halves_body(place_ref, w_ref, _, own_ref, away_ref, token_ref, sems):
    token_ref[...] = jnp.zeros_like(token_ref)
    half = own_ref.shape[1]
    core = place_ref[1]
    copies = [
        pltpu.make_async_copy(w_ref.at[:, pl.ds(pl.multiple_of(side * half, 128), half)], out, sems.at[i])
        for i, (side, out) in enumerate(((core, own_ref), (1 - core, away_ref)))
    ]
    for c in copies:
        c.start()
    for c in copies:
        c.wait()


def halves(weights, place, after):
    rows, width = weights.shape
    shape = jax.ShapeDtypeStruct((rows, width // 2), BF16)
    return pl.pallas_call(
        halves_body,
        in_specs=[SMEM, HBM, ANY],
        out_specs=[VMEM] * 3,
        out_shape=[shape] * 2 + [TOKEN],
        scratch_shapes=[pltpu.SemaphoreType.DMA((2,))],
        compiler_params=params(2),
        cost_estimate=QUICK,
        name="halves",
    )(place, pltpu.with_memory_space_constraint(weights, pltpu.HBM), after)


def rows_body(count, shift, place_ref, *refs):
    core = place_ref[1]
    out = refs[-1]
    rows = out.shape[0]
    side = core if shift == 0 else 1 - core
    at = pl.multiple_of(side * rows, rows)
    width = refs[0].shape[1]
    for i in range(count):
        out[:, i * width : (i + 1) * width] = refs[i][pl.ds(at, rows), :]


def core_rows(chunks, place, shift):
    rows = chunks[0].shape[0] // 2
    width = sum(c.shape[1] for c in chunks)
    return pl.pallas_call(
        functools.partial(rows_body, len(chunks), shift),
        in_specs=[SMEM] + [VMEM] * len(chunks),
        out_specs=VMEM,
        out_shape=jax.ShapeDtypeStruct((rows, width), BF16),
        compiler_params=params(4),
        cost_estimate=QUICK,
        name="core_rows",
    )(place, *chunks)


def join_body(place_ref, near_ref, far_ref, out_ref):
    half = near_ref.shape[1]
    own = place_ref[1] == 0
    near, far = near_ref[...], far_ref[...]
    out_ref[:, :half] = jnp.where(own, near, far)
    out_ref[:, half:] = jnp.where(own, far, near)


def join(near, far, place):
    rows, half = near.shape
    return pl.pallas_call(
        join_body,
        in_specs=[SMEM, VMEM, VMEM],
        out_specs=VMEM,
        out_shape=jax.ShapeDtypeStruct((rows, 2 * half), BF16),
        compiler_params=params(4),
        cost_estimate=QUICK,
        name="join",
    )(place, near, far)


def project_part(pieces, part, w_ref, down_ref, rows_ref, acc_ref, lat_ref, acc, lat):
    at = 0
    for piece in pieces:
        rows_ref[at : at + piece.shape[0], :] = piece[...]
        at += piece.shape[0]
    width = rows_ref.shape[1]
    kb = width // 4
    for s in range(4):
        x = rows_ref[:, s * kb : (s + 1) * kb]
        k = part * width + s * kb
        more = lax.dot_general(w_ref[:, k : k + kb], x, NT, preferred_element_type=F32)
        extra = jnp.dot(x, down_ref[k : k + kb, :], preferred_element_type=F32)
        if s == 0 and acc is None:
            acc_ref[...] = more
            lat_ref[...] = extra
        elif s == 0:
            acc_ref[...] = acc[...] + more
            lat_ref[...] = lat[...] + extra
        else:
            acc_ref[...] += more
            lat_ref[...] += extra


def project_body(count, ties, *refs):
    pieces = refs[:count]
    w_ref, down_ref, acc_ref, lat_ref, rows_ref = refs[count : count + 2] + refs[count + 2 + ties :]
    project_part(pieces, 0, w_ref, down_ref, rows_ref, acc_ref, lat_ref, None, None)


def attend_body(count, blocks, dims, place_ref, len_ref, *refs):
    pieces = refs[:count]
    kv_refs = refs[count : count + blocks]
    w_ref, down_ref, up_ref, acc_in, lat_in, out_ref, rows_ref, acc_ref, lat_ref = refs[count + blocks :]
    rows, cols, chips, tok_dev = dims
    project_part(pieces, 1, w_ref, down_ref, rows_ref, acc_ref, lat_ref, acc_in, lat_in)

    chip, core = place_ref[0], place_ref[1]
    keys_t = acc_ref[cols : 2 * cols, :].astype(BF16)
    vals_t = acc_ref[2 * cols :, :].astype(BF16)
    cached_k = jnp.concatenate([kv[s, 0] for kv in kv_refs for s in range(2)], axis=0)
    cached_v = jnp.concatenate([kv[s, 1] for kv in kv_refs for s in range(2)], axis=0)
    up = up_ref[...]
    scale = HD ** (-0.5)
    pair = 2 * tok_dev

    def spots(row):
        slot = row // pair
        inside = row - slot * pair
        side = inside // tok_dev
        owner = chip - slot
        owner = jnp.where(owner < 0, owner + chips, owner)
        at = jnp.where(core == 0, side, 1 - side)
        return owner * pair + at * tok_dev + inside - side * tok_dev

    def requests(spot):
        end = len_ref[0, 0]
        found = (spot >= end).astype(jnp.int32)
        for j in range(1, len_ref.shape[1]):
            end = end + len_ref[0, j]
            found = found + (spot >= end).astype(jnp.int32)
        return found

    block = min(256, rows)
    key_spot = spots(lax.broadcasted_iota(jnp.int32, (rows, 1), 0))
    key_req = requests(key_spot)

    def one_block(b, carry):
        r0 = pl.multiple_of(b * block, block)
        lat = lat_ref[pl.ds(r0, block), :].astype(BF16)
        q = acc_ref[:cols, pl.ds(r0, block)] + lax.dot_general(up, lat, NT, preferred_element_type=F32)
        q = q.astype(BF16)
        q_spot = spots(r0 + lax.broadcasted_iota(jnp.int32, (1, block), 1))
        allowed = jnp.logical_and(requests(q_spot) == key_req, key_spot <= q_spot)
        pre = jnp.dot(cached_k, q, preferred_element_type=F32) * scale
        suf = lax.dot_general(keys_t, q, TN, preferred_element_type=F32) * scale
        suf = jnp.where(allowed, suf, -jnp.inf)
        top = jnp.maximum(jnp.max(pre, axis=0, keepdims=True), jnp.max(suf, axis=0, keepdims=True))
        pre = jnp.exp(pre - top)
        suf = jnp.exp(suf - top)
        total = jnp.sum(pre, axis=0, keepdims=True) + jnp.sum(suf, axis=0, keepdims=True)
        weighted = lax.dot_general(cached_v, pre.astype(BF16), TN, preferred_element_type=F32) + jnp.dot(
            vals_t, suf.astype(BF16), preferred_element_type=F32
        )
        heads = (weighted / total).T.astype(BF16)
        for k in range(block // tok_dev):
            base = r0 + (k // 2) * pair
            shift = (core if k % 2 == 0 else 1 - core) * tok_dev
            at = pl.multiple_of(base + shift, tok_dev)
            out_ref[pl.ds(at, tok_dev), :] = heads[k * tok_dev : (k + 1) * tok_dev]
        return carry

    if rows == block:
        one_block(0, 0)
    else:
        lax.fori_loop(0, rows // block, one_block, 0)


def project(pieces, w_t, down, ties):
    rows = sum(p.shape[0] for p in pieces)
    width = pieces[0].shape[1]
    cols3, rank = w_t.shape[0], down.shape[1]
    return pl.pallas_call(
        functools.partial(project_body, len(pieces), len(ties)),
        in_specs=[VMEM] * (len(pieces) + 2) + [ANY] * len(ties),
        out_specs=[VMEM] * 2,
        out_shape=[jax.ShapeDtypeStruct((cols3, rows), F32), jax.ShapeDtypeStruct((rows, rank), F32)],
        scratch_shapes=[pltpu.VMEM((rows, width), BF16)],
        compiler_params=params(6 + rows * width * 4 // 2**20),
        cost_estimate=QUICK,
        name="project",
    )(*pieces, w_t, down, *ties)


def attend(pieces, w_t, down, up_t, kv_blocks, acc, lat, place, lengths, chips):
    rows = sum(p.shape[0] for p in pieces)
    width = pieces[0].shape[1]
    cols3, rank = w_t.shape[0], down.shape[1]
    cols = cols3 // 3
    dims = (rows, cols, chips, pieces[0].shape[0])
    return pl.pallas_call(
        functools.partial(attend_body, len(pieces), len(kv_blocks), dims),
        in_specs=[SMEM, SMEM] + [VMEM] * (len(pieces) + len(kv_blocks) + 5),
        out_specs=VMEM,
        out_shape=jax.ShapeDtypeStruct((rows, cols), BF16),
        scratch_shapes=[
            pltpu.VMEM((rows, width), BF16),
            pltpu.VMEM((cols3, rows), F32),
            pltpu.VMEM((rows, rank), F32),
        ],
        compiler_params=params(10 + rows * width * 5 // 2**20),
        cost_estimate=QUICK,
        name="attend",
    )(place, lengths, *pieces, *kv_blocks, w_t, down, up_t, acc, lat)


def out_body(a_ref, b_ref, wa_ref, wb_ref, out_ref):
    out_ref[...] = jnp.dot(a_ref[...], wa_ref[...], preferred_element_type=F32) + jnp.dot(
        b_ref[...], wb_ref[...], preferred_element_type=F32
    )


def out_project(own, got, w_own, w_got):
    rows, width = own.shape[0], w_own.shape[1]
    return pl.pallas_call(
        out_body,
        in_specs=[VMEM] * 4,
        out_specs=VMEM,
        out_shape=jax.ShapeDtypeStruct((rows, width), F32),
        compiler_params=params(4 + rows * width * 8 // 2**20),
        cost_estimate=QUICK,
        name="out_project",
    )(own, got, w_own, w_got)


def add_body(row, col, got_ref, part_ref, *rest):
    rows, width = got_ref.shape
    out_ref = rest[-1]
    total = got_ref[...].astype(F32) + part_ref[row : row + rows, col : col + width]
    out_ref[...] = total.astype(BF16)


def add_slot(got, partial, row, col, ties=()):
    return pl.pallas_call(
        functools.partial(add_body, row, col),
        in_specs=[VMEM] * 2 + [ANY] * len(ties),
        out_specs=VMEM,
        out_shape=jax.ShapeDtypeStruct(got.shape, BF16),
        compiler_params=params(4),
        cost_estimate=QUICK,
        name="add_slot",
    )(got, partial, *ties)


def finish_body(count, place_ref, part_ref, *refs):
    gots = refs[:count]
    near_ref, far_ref = refs[-2:]
    core = place_ref[1]
    rows = near_ref.shape[0]
    width = gots[0].shape[1]
    for out, side in ((near_ref, core), (far_ref, 1 - core)):
        at = pl.multiple_of(side * rows, rows)
        for i, got in enumerate(gots):
            cols = slice(i * width, (i + 1) * width)
            total = got[pl.ds(at, rows), :].astype(F32) + part_ref[pl.ds(at, rows), cols]
            out[:, cols] = total.astype(BF16)


def finish(gots, partial, place):
    rows = gots[0].shape[0] // 2
    shape = jax.ShapeDtypeStruct((rows, partial.shape[1]), BF16)
    return pl.pallas_call(
        functools.partial(finish_body, len(gots)),
        in_specs=[SMEM] + [VMEM] * (1 + len(gots)),
        out_specs=[VMEM] * 2,
        out_shape=[shape] * 2,
        compiler_params=params(4),
        cost_estimate=QUICK,
        name="finish",
    )(place, partial, *gots)


def gate_body(count, dims, place_ref, gain_ref, *refs):
    slots, chunks, parts = dims
    pieces = refs[:count]
    weights = refs[count : count + parts]
    down_ref, out_ref, away_ref, x_ref = refs[count + parts :]
    core = place_ref[1]
    half = x_ref.shape[2]
    tile = tile_of(out_ref.shape[1])
    steps = out_ref.shape[1] // tile

    low, high = gain_ref[:half].reshape(1, half), gain_ref[half:].reshape(1, half)
    own_gain = jnp.where(core == 0, low, high)
    got_gain = jnp.where(core == 0, high, low)
    at = iter(pieces)
    row = 0
    for _k in range(slots):
        own = [next(at)[...].astype(F32) for _c in range(chunks)]
        got = [next(at)[...].astype(F32) for _c in range(chunks)]
        own = jnp.concatenate(own, axis=1)
        got = jnp.concatenate(got, axis=1)
        n = own.shape[0]
        square = jnp.sum(own * own, axis=-1, keepdims=True) + jnp.sum(got * got, axis=-1, keepdims=True)
        scale = lax.rsqrt(square * (0.5 / half) + EPS)
        x_ref[core, row : row + n, :] = (own * scale * own_gain).astype(BF16)
        x_ref[1 - core, row : row + n, :] = (got * scale * got_gain).astype(BF16)
        row += n

    per = half * 2 // parts
    for j in range(steps):
        gate = up = None
        for p in range(parts):
            side, at = divmod(p * per, half)
            x = x_ref[side, :, at : at + per]
            g = jnp.dot(x, weights[p][0, :, j * tile : (j + 1) * tile], preferred_element_type=F32)
            u = jnp.dot(x, weights[p][1, :, j * tile : (j + 1) * tile], preferred_element_type=F32)
            gate = g if gate is None else gate + g
            up = u if up is None else up + u
        out_ref[:, j * tile : (j + 1) * tile] = (gate / (1.0 + jnp.exp(-gate)) * up).astype(BF16)

    hidden = out_ref[...]
    wide = tile_of(half)
    for j in range(0, half, wide):
        away_ref[:, j : j + wide] = jnp.dot(hidden, down_ref[:, j : j + wide], preferred_element_type=F32).astype(BF16)


def gate_up(pieces, slots, chunks, weights, down, gain, place):
    half = gain.shape[0] // 2
    rows = slots * pieces[0].shape[0]
    parts = len(weights)
    units = weights[0].shape[2]
    return pl.pallas_call(
        functools.partial(gate_body, len(pieces), (slots, chunks, parts)),
        in_specs=[SMEM] + [VMEM] * (2 + len(pieces) + parts),
        out_specs=[VMEM] * 2,
        out_shape=[jax.ShapeDtypeStruct((rows, units), BF16), jax.ShapeDtypeStruct((rows, half), BF16)],
        scratch_shapes=[pltpu.VMEM((2, rows, half), BF16)],
        compiler_params=params(3 + rows * half * 18 // 2**20),
        cost_estimate=QUICK,
        name="gate_up",
    )(place, gain, *pieces, *weights, down)


def down_body(x_ref, w_ref, got_ref, out_ref):
    half = out_ref.shape[1]
    wide = tile_of(half)
    x = x_ref[...]
    for j in range(0, half, wide):
        out_ref[:, j : j + wide] = jnp.dot(x, w_ref[:, j : j + wide], preferred_element_type=F32)


def down_half(hidden, down):
    rows, units = hidden.shape
    half = down.shape[1]
    return pl.pallas_call(
        lambda x_ref, w_ref, out_ref: down_body(x_ref, w_ref, None, out_ref),
        in_specs=[VMEM] * 2,
        out_specs=VMEM,
        out_shape=jax.ShapeDtypeStruct((rows, half), F32),
        compiler_params=params(4 + rows * half * 4 // 2**20),
        cost_estimate=QUICK,
        name="down_half",
    )(hidden, down)


def make(mesh):
    n = mesh.shape["hid"]
    n_req = mesh.shape["req"]
    chips = n // 2
    both = [(h, h ^ 1) for h in range(n)]
    ring = [(h, (h + 2) % n) for h in range(n)]

    def swap(v):
        return lax.ppermute(v, "hid", both)

    def onward(v):
        return lax.ppermute(v, "hid", ring)

    def gather(own, fillers=()):
        slots = [list(own)]
        here = list(own)
        gave = []
        fillers = list(fillers)
        for k in range(1, chips):
            done = [fillers.pop(0)(here[-1])] if fillers else []
            here = [onward(v) for v in here]
            for what, token in done:
                here = [pass_on(v, token) for v in here]
                gave.append(what)
            slots.append(here)
        gave += [f(here[-1])[0] for f in fillers]
        return [(s, [swap(v) for v in s]) for s in slots], gave

    def scatter(partial, count, fillers=(), place=None):
        rows = partial.shape[0] // chips
        width = partial.shape[1] // count
        sums = [partial[rows : 2 * rows, i * width : (i + 1) * width].astype(BF16) for i in range(count)]
        gave = []
        fillers = list(fillers)
        for k in range(2, chips + 1):
            done = [fillers.pop(0)(sums[-1])] if fillers else []
            ties = [d[1] for d in done]
            gave += [d[0] for d in done]
            sums = [onward(v) for v in sums]
            if k == chips and place is not None:
                return finish(sums, partial, place), gave
            sums = [add_slot(v, partial, k % chips * rows, i * width, ties) for i, v in enumerate(sums)]
        gave += [f(sums[-1])[0] for f in fillers]
        return sums, gave

    def per_device(tokens, gain_in, w_qkv, adapt_down, adapt_up, w_out, gain_ff, w_gate_up, w_down,
                   prefix_cache, prefix_owner, group_prefix, lengths):
        tok_dev, width_in = tokens.shape
        cols = w_qkv.shape[2]
        model_width = w_out.shape[1]
        half = model_width // 2
        hid = lax.axis_index("hid")
        req = lax.axis_index("req")
        core = hid % 2
        chip = hid // 2
        place = jnp.stack([chip, core, req]).astype(jnp.int32)

        here = norm_rows(tokens, gain_in[None, :], 2)
        w_t = jnp.transpose(w_qkv, (1, 2, 0)).reshape(3 * cols, width_in)

        def hold_weights(v):
            *held, token = hold(w_t, adapt_down, place, v)
            return held, token

        def split_out(v):
            *sides, token = halves(w_out, place, v)
            return sides, token

        def cached(v):
            mine, other = split_heads(candidates, place, prefix_owner, group_prefix, chips, [v])
            blocks = pack_blocks(mine, swap(other), place)
            return blocks, blocks[0]

        cache = prefix_cache[0]
        candidates = [cache] + [
            lax.ppermute(cache, "req", [(r, r ^ k) for r in range(n_req)]) for k in range(1, n_req)
        ]
        slots, given = gather(here, [hold_weights, split_out, cached])
        (w_t, adapt_down), (w_own, w_away), kv_blocks = given
        kv_blocks = [
            lax.ppermute(block, "hid", [(h, h ^ (2 * k)) for h in range(n)]) if k else block
            for k, block in enumerate(kv_blocks)
        ]
        w_got = swap(w_away)

        pick = lambda i: [v for s in slots for v in (s[0][i], s[1][i])]
        acc, lat = project(pick(0), w_t, adapt_down, kv_blocks[1:])
        heads = attend(pick(1), w_t, adapt_down, adapt_up.T, kv_blocks, acc, lat, place, lengths, chips)
        partial = out_project(heads, swap(heads), w_own, w_got)

        parts = 4
        work = [lambda v, p=p: unpair(w_gate_up, p, parts, v) for p in range(parts)]
        work += [lambda v, flip=flip: bring(w_down, place, flip, v) for flip in (True, False)]
        sums, early = scatter(partial, 2, work[:3])
        summed, late = gather(sums, work[3:])
        *w_pairs, down_away, down_own = early + late

        def first_output(_):
            attn_own = join(core_rows(summed[0][0], place, 0), core_rows(summed[0][1], place, 0), place)
            return attn_own, attn_own

        pieces = [v for s in summed for v in s[0] + s[1]]
        hidden, away_half = gate_up(pieces, chips, 2, w_pairs, down_away, gain_ff, place)
        got_half = swap(away_half)
        own_half = down_half(hidden, down_own)
        ends, (attn_own,) = scatter(own_half + got_half.astype(F32), 2, [first_output], place)
        block_own = join(ends[0], swap(ends[1]), place)
        return attn_own, block_own

    return per_device


def solution(mesh):
    placed = (
        P(("req", "hid"), None),
        P(),
        P(None, None, "hid"),
        P(),
        P(None, "hid"),
        P("hid", None),
        P(),
        P(None, None, "hid"),
        P("hid", None),
        P("req", "hid", None, None),
        P(),
        P(),
        P("req", None),
    )
    return jax.shard_map(
        make(mesh),
        mesh=mesh,
        in_specs=placed,
        out_specs=(P(("req", "hid"), None), P(("req", "hid"), None)),
        check_vma=False,
    )
```

```python
import functools

import jax
import jax.numpy as jnp
from jax import lax
from jax.experimental import pallas as pl
from jax.experimental.pallas import tpu as pltpu
from jax.sharding import PartitionSpec as P

HD = 224
EPS = 1e-05
EARLY = 1
CUTS = (1, 2, 4)
F32 = jnp.float32
BF16 = jnp.bfloat16
NT = (((1,), (1,)), ((), ()))
TN = (((0,), (0,)), ((), ()))
VMEM = pl.BlockSpec(memory_space=pltpu.VMEM)
SMEM = pl.BlockSpec(memory_space=pltpu.SMEM)
ANY = pl.BlockSpec(memory_space=pl.ANY)
TOKEN = jax.ShapeDtypeStruct((8, 128), F32)
QUICK = pl.CostEstimate(flops=1, bytes_accessed=1, transcendentals=0)
HBM = pl.BlockSpec(memory_space=pltpu.HBM)


def params(mib=56):
    return pltpu.CompilerParams(vmem_limit_bytes=mib * 2**20)


def split_cols(block, count):
    width = block.shape[1] // count
    return [block[:, i * width : (i + 1) * width] for i in range(count)]


def tile_of(width):
    return 256 if width % 256 == 0 else width


def norm_body(tok_ref, gain_ref, *outs):
    t = tok_ref[...].astype(F32)
    scale = lax.rsqrt(jnp.mean(t * t, axis=-1, keepdims=True) + EPS)
    normed = (t * scale * gain_ref[...]).astype(BF16)
    width = t.shape[1] // len(outs)
    for i, out in enumerate(outs):
        out[...] = normed[:, i * width : (i + 1) * width]


def norm_rows(tokens, gain, count):
    rows, width = tokens.shape
    return pl.pallas_call(
        norm_body,
        in_specs=[VMEM, VMEM],
        out_specs=[VMEM] * count,
        out_shape=[jax.ShapeDtypeStruct((rows, width // count), BF16)] * count,
        compiler_params=params(16),
        cost_estimate=QUICK,
        name="norm_rows",
    )(tokens, gain)


def unpair_body(first, w_ref, _, out_ref, token_ref, buf, sems):
    token_ref[...] = jnp.zeros_like(token_ref)
    count, step = buf.shape[:2]

    def fetch(i):
        return pltpu.make_async_copy(w_ref.at[pl.ds(first + i * step, step)], buf.at[i], sems.at[i])

    for i in range(count):
        fetch(i).start()
    for i in range(count):
        fetch(i).wait()
        out_ref[:, i * step : (i + 1) * step, :] = jnp.swapaxes(buf[i], 0, 1)


def unpair(weights, first, rows, after):
    _, two, width = weights.shape
    count = 4
    step = rows // count
    return pl.pallas_call(
        functools.partial(unpair_body, first),
        in_specs=[HBM, ANY],
        out_specs=[VMEM] * 2,
        out_shape=[jax.ShapeDtypeStruct((two, rows, width), BF16), TOKEN],
        scratch_shapes=[pltpu.VMEM((count, step, two, width), BF16), pltpu.SemaphoreType.DMA((count,))],
        compiler_params=params(11),
        cost_estimate=QUICK,
        name="unpair",
    )(pltpu.with_memory_space_constraint(weights, pltpu.HBM), after)


def hold_body(place_ref, w_ref, down_ref, _, w_out, down_out, token_ref, sems):
    token_ref[...] = jnp.zeros_like(token_ref)
    copies = [pltpu.make_async_copy(down_ref, down_out, sems.at[0])]
    count = sems.shape[0] - 1
    step = w_ref.shape[0] // count
    for i in range(count):
        rows = pl.ds(i * step, step)
        copies.append(pltpu.make_async_copy(w_ref.at[rows], w_out.at[rows], sems.at[1 + i]))
    for c in copies:
        c.start()
    for c in copies:
        c.wait()


def hold(w_t, down, place, after):
    return pl.pallas_call(
        hold_body,
        in_specs=[SMEM, HBM, HBM, ANY],
        out_specs=[VMEM] * 3,
        out_shape=[jax.ShapeDtypeStruct(w_t.shape, BF16), jax.ShapeDtypeStruct(down.shape, BF16), TOKEN],
        scratch_shapes=[pltpu.SemaphoreType.DMA((7,))],
        compiler_params=params(2),
        cost_estimate=QUICK,
        name="hold",
    )(place, pltpu.with_memory_space_constraint(w_t, pltpu.HBM), pltpu.with_memory_space_constraint(down, pltpu.HBM), after)


def bring_body(flip, place_ref, w_ref, _, out_ref, token_ref, sems):
    token_ref[...] = jnp.zeros_like(token_ref)
    units, half = out_ref.shape
    core = place_ref[1]
    at = pl.multiple_of((1 - core if flip else core) * half, 128)
    count = sems.shape[0]
    step = units // count

    def fetch(i):
        rows = pl.ds(i * step, step)
        return pltpu.make_async_copy(w_ref.at[rows, pl.ds(at, half)], out_ref.at[rows], sems.at[i])

    for i in range(count):
        fetch(i).start()
    for i in range(count):
        fetch(i).wait()


def bring(w_down, place, flip, after):
    units, width = w_down.shape
    return pl.pallas_call(
        functools.partial(bring_body, flip),
        in_specs=[SMEM, HBM, ANY],
        out_specs=[VMEM] * 2,
        out_shape=[jax.ShapeDtypeStruct((units, width // 2), BF16), TOKEN],
        scratch_shapes=[pltpu.SemaphoreType.DMA((8,))],
        compiler_params=params(2),
        cost_estimate=QUICK,
        name="bring",
    )(place, pltpu.with_memory_space_constraint(w_down, pltpu.HBM), after)


def pass_body(*_refs):
    pass


def pass_on(value, tokens):
    return pl.pallas_call(
        pass_body,
        in_specs=[ANY] * (1 + len(tokens)),
        out_specs=ANY,
        out_shape=jax.ShapeDtypeStruct(value.shape, value.dtype),
        input_output_aliases={0: 0},
        compiler_params=params(1),
        cost_estimate=QUICK,
        name="pass_on",
    )(value, *tokens)


def split_body(count, place_ref, owner_ref, group_ref, *refs):
    candidates = refs[:count]
    mine_ref, other_ref = refs[-2:]
    core, req = place_ref[1], place_ref[2]
    away = owner_ref[group_ref[req]] ^ req
    chips = mine_ref.shape[0]
    cols = mine_ref.shape[3]
    chosen = candidates[0][...]
    for k in range(1, count):
        chosen = jnp.where(away == k, candidates[k][...], chosen)
    chosen = jnp.swapaxes(chosen, 0, 1)
    for c in range(chips):
        even = chosen[:, :, 2 * c * cols : (2 * c + 1) * cols]
        odd = chosen[:, :, (2 * c + 1) * cols : (2 * c + 2) * cols]
        mine_ref[c] = jnp.where(core == 0, even, odd)
        other_ref[c] = jnp.where(core == 0, odd, even)


def split_heads(candidates, place, owner, group, chips, ties):
    positions, two, width = candidates[0].shape
    shape = jax.ShapeDtypeStruct((chips, two, positions, width // (2 * chips)), BF16)
    return pl.pallas_call(
        functools.partial(split_body, len(candidates)),
        in_specs=[SMEM] * 3 + [VMEM] * len(candidates) + [ANY] * len(ties),
        out_specs=[VMEM] * 2,
        out_shape=[shape] * 2,
        compiler_params=params(16),
        cost_estimate=QUICK,
        name="split_heads",
    )(place, owner, group, *candidates, *ties)


def pack_body(place_ref, mine_ref, got_ref, *outs):
    chip = place_ref[0]
    for k, out in enumerate(outs):
        out[0] = mine_ref[chip ^ k]
        out[1] = got_ref[chip ^ k]


def pack_blocks(mine, got, place):
    chips = mine.shape[0]
    shape = jax.ShapeDtypeStruct((2, *mine.shape[1:]), BF16)
    return pl.pallas_call(
        pack_body,
        in_specs=[SMEM, VMEM, VMEM],
        out_specs=[VMEM] * chips,
        out_shape=[shape] * chips,
        compiler_params=params(4),
        cost_estimate=QUICK,
        name="pack_blocks",
    )(place, mine, got)


def halves_body(place_ref, w_ref, _, own_ref, away_ref, token_ref, sems):
    token_ref[...] = jnp.zeros_like(token_ref)
    half = own_ref.shape[1]
    core = place_ref[1]
    copies = [
        pltpu.make_async_copy(w_ref.at[:, pl.ds(pl.multiple_of(side * half, 128), half)], out, sems.at[i])
        for i, (side, out) in enumerate(((core, own_ref), (1 - core, away_ref)))
    ]
    for c in copies:
        c.start()
    for c in copies:
        c.wait()


def halves(weights, place, after):
    rows, width = weights.shape
    shape = jax.ShapeDtypeStruct((rows, width // 2), BF16)
    return pl.pallas_call(
        halves_body,
        in_specs=[SMEM, HBM, ANY],
        out_specs=[VMEM] * 3,
        out_shape=[shape] * 2 + [TOKEN],
        scratch_shapes=[pltpu.SemaphoreType.DMA((2,))],
        compiler_params=params(2),
        cost_estimate=QUICK,
        name="halves",
    )(place, pltpu.with_memory_space_constraint(weights, pltpu.HBM), after)


def rows_body(count, place_ref, *refs):
    core = place_ref[1]
    out = refs[-1]
    step = refs[0].shape[0]
    for i in range(count // 2):
        out[i * step : (i + 1) * step, :] = jnp.where(core == 0, refs[i][...], refs[count // 2 + i][...])


def core_rows(chunks, place):
    step, width = chunks[0].shape
    count = len(chunks)
    return pl.pallas_call(
        functools.partial(rows_body, count),
        in_specs=[SMEM] + [VMEM] * count,
        out_specs=VMEM,
        out_shape=jax.ShapeDtypeStruct((step * count // 2, width), BF16),
        compiler_params=params(4),
        cost_estimate=QUICK,
        name="core_rows",
    )(place, *chunks)


def join_body(place_ref, near_ref, far_ref, out_ref):
    half = near_ref.shape[1]
    own = place_ref[1] == 0
    near, far = near_ref[...], far_ref[...]
    out_ref[:, :half] = jnp.where(own, near, far)
    out_ref[:, half:] = jnp.where(own, far, near)


def join(near, far, place):
    rows, half = near.shape
    return pl.pallas_call(
        join_body,
        in_specs=[SMEM, VMEM, VMEM],
        out_specs=VMEM,
        out_shape=jax.ShapeDtypeStruct((rows, 2 * half), BF16),
        compiler_params=params(4),
        cost_estimate=QUICK,
        name="join",
    )(place, near, far)


def project_part(pieces, part, w_ref, down_ref, rows_ref, acc_ref, lat_ref, acc, lat):
    at = 0
    for piece in pieces:
        rows_ref[at : at + piece.shape[0], :] = piece[...]
        at += piece.shape[0]
    width = rows_ref.shape[1]
    kb = width // 4
    for s in range(4):
        x = rows_ref[:, s * kb : (s + 1) * kb]
        k = part * width + s * kb
        more = lax.dot_general(w_ref[:, k : k + kb], x, NT, preferred_element_type=F32)
        extra = jnp.dot(x, down_ref[k : k + kb, :], preferred_element_type=F32)
        if s == 0 and acc is None:
            acc_ref[...] = more
            lat_ref[...] = extra
        elif s == 0:
            acc_ref[...] = acc[...] + more
            lat_ref[...] = lat[...] + extra
        else:
            acc_ref[...] += more
            lat_ref[...] += extra


def project_body(count, ties, *refs):
    pieces = refs[:count]
    w_ref, down_ref, acc_ref, lat_ref, rows_ref = refs[count : count + 2] + refs[count + 2 + ties :]
    project_part(pieces, 0, w_ref, down_ref, rows_ref, acc_ref, lat_ref, None, None)


def attend_body(count, blocks, dims, place_ref, len_ref, *refs):
    pieces = refs[:count]
    kv_refs = refs[count : count + blocks]
    w_ref, down_ref, up_ref, acc_in, lat_in, out_ref, rows_ref, acc_ref, lat_ref = refs[count + blocks :]
    rows, cols, chips, tok_dev = dims
    project_part(pieces, 1, w_ref, down_ref, rows_ref, acc_ref, lat_ref, acc_in, lat_in)

    chip, core = place_ref[0], place_ref[1]
    keys_t = acc_ref[cols : 2 * cols, :].astype(BF16)
    vals_t = acc_ref[2 * cols :, :].astype(BF16)
    cached_k = jnp.concatenate([kv[s, 0] for kv in kv_refs for s in range(2)], axis=0)
    cached_v = jnp.concatenate([kv[s, 1] for kv in kv_refs for s in range(2)], axis=0)
    up = up_ref[...]
    scale = HD ** (-0.5)
    pair = 2 * tok_dev

    def spots(row):
        slot = row // pair
        inside = row - slot * pair
        side = inside // tok_dev
        owner = chip - slot
        owner = jnp.where(owner < 0, owner + chips, owner)
        at = jnp.where(core == 0, side, 1 - side)
        return owner * pair + at * tok_dev + inside - side * tok_dev

    def requests(spot):
        end = len_ref[0, 0]
        found = (spot >= end).astype(jnp.int32)
        for j in range(1, len_ref.shape[1]):
            end = end + len_ref[0, j]
            found = found + (spot >= end).astype(jnp.int32)
        return found

    block = min(256, rows)
    key_spot = spots(lax.broadcasted_iota(jnp.int32, (rows, 1), 0))
    key_req = requests(key_spot)

    def one_block(b, carry):
        r0 = pl.multiple_of(b * block, block)
        lat = lat_ref[pl.ds(r0, block), :].astype(BF16)
        q = acc_ref[:cols, pl.ds(r0, block)] + lax.dot_general(up, lat, NT, preferred_element_type=F32)
        q = q.astype(BF16)
        q_spot = spots(r0 + lax.broadcasted_iota(jnp.int32, (1, block), 1))
        allowed = jnp.logical_and(requests(q_spot) == key_req, key_spot <= q_spot)
        pre = jnp.dot(cached_k, q, preferred_element_type=F32) * scale
        suf = lax.dot_general(keys_t, q, TN, preferred_element_type=F32) * scale
        suf = jnp.where(allowed, suf, -jnp.inf)
        top = jnp.maximum(jnp.max(pre, axis=0, keepdims=True), jnp.max(suf, axis=0, keepdims=True))
        pre = jnp.exp(pre - top)
        suf = jnp.exp(suf - top)
        total = jnp.sum(pre, axis=0, keepdims=True) + jnp.sum(suf, axis=0, keepdims=True)
        weighted = lax.dot_general(cached_v, pre.astype(BF16), TN, preferred_element_type=F32) + jnp.dot(
            vals_t, suf.astype(BF16), preferred_element_type=F32
        )
        heads = (weighted / total).T.astype(BF16)
        for k in range(block // tok_dev):
            base = r0 + (k // 2) * pair
            shift = (core if k % 2 == 0 else 1 - core) * tok_dev
            at = pl.multiple_of(base + shift, tok_dev)
            out_ref[pl.ds(at, tok_dev), :] = heads[k * tok_dev : (k + 1) * tok_dev]
        return carry

    if rows == block:
        one_block(0, 0)
    else:
        lax.fori_loop(0, rows // block, one_block, 0)


def project(pieces, w_t, down, ties):
    rows = sum(p.shape[0] for p in pieces)
    width = pieces[0].shape[1]
    cols3, rank = w_t.shape[0], down.shape[1]
    return pl.pallas_call(
        functools.partial(project_body, len(pieces), len(ties)),
        in_specs=[VMEM] * (len(pieces) + 2) + [ANY] * len(ties),
        out_specs=[VMEM] * 2,
        out_shape=[jax.ShapeDtypeStruct((cols3, rows), F32), jax.ShapeDtypeStruct((rows, rank), F32)],
        scratch_shapes=[pltpu.VMEM((rows, width), BF16)],
        compiler_params=params(6 + rows * width * 4 // 2**20),
        cost_estimate=QUICK,
        name="project",
    )(*pieces, w_t, down, *ties)


def attend(pieces, w_t, down, up_t, kv_blocks, acc, lat, place, lengths, chips):
    rows = sum(p.shape[0] for p in pieces)
    width = pieces[0].shape[1]
    cols3, rank = w_t.shape[0], down.shape[1]
    cols = cols3 // 3
    dims = (rows, cols, chips, pieces[0].shape[0])
    return pl.pallas_call(
        functools.partial(attend_body, len(pieces), len(kv_blocks), dims),
        in_specs=[SMEM, SMEM] + [VMEM] * (len(pieces) + len(kv_blocks) + 5),
        out_specs=VMEM,
        out_shape=jax.ShapeDtypeStruct((rows, cols), BF16),
        scratch_shapes=[
            pltpu.VMEM((rows, width), BF16),
            pltpu.VMEM((cols3, rows), F32),
            pltpu.VMEM((rows, rank), F32),
        ],
        compiler_params=params(10 + rows * width * 5 // 2**20),
        cost_estimate=QUICK,
        name="attend",
    )(place, lengths, *pieces, *kv_blocks, w_t, down, up_t, acc, lat)


def out_body(a_ref, b_ref, wa_ref, wb_ref, out_ref):
    out_ref[...] = jnp.dot(a_ref[...], wa_ref[...], preferred_element_type=F32) + jnp.dot(
        b_ref[...], wb_ref[...], preferred_element_type=F32
    )


def out_project(own, got, w_own, w_got):
    rows, width = own.shape[0], w_own.shape[1]
    return pl.pallas_call(
        out_body,
        in_specs=[VMEM] * 4,
        out_specs=VMEM,
        out_shape=jax.ShapeDtypeStruct((rows, width), F32),
        compiler_params=params(4 + rows * width * 8 // 2**20),
        cost_estimate=QUICK,
        name="out_project",
    )(own, got, w_own, w_got)


def add_body(row, got_ref, part_ref, *rest):
    rows = got_ref.shape[0]
    out_ref = rest[-1]
    out_ref[...] = (got_ref[...].astype(F32) + part_ref[row : row + rows, :]).astype(BF16)


def add_slot(got, partial, row, ties=()):
    return pl.pallas_call(
        functools.partial(add_body, row),
        in_specs=[VMEM] * 2 + [ANY] * len(ties),
        out_specs=VMEM,
        out_shape=jax.ShapeDtypeStruct(got.shape, BF16),
        compiler_params=params(4),
        cost_estimate=QUICK,
        name="add_slot",
    )(got, partial, *ties)


def finish_body(ties, by_core, place_ref, part_ref, *refs):
    gots, outs = refs[:4], refs[4 + ties :]
    step = gots[0].shape[0]
    sums = []
    for i in range(2):
        total = part_ref[i * step : (i + 1) * step, :]
        total = total + gots[i][...].astype(F32) + gots[2 + i][...].astype(F32)
        sums.append(total.astype(BF16))
    if by_core:
        own = place_ref[1] == 0
        sums = [jnp.where(own, sums[0], sums[1]), jnp.where(own, sums[1], sums[0])]
    for out, value in zip(outs, sums):
        out[...] = value


def finish(ahead, behind, partial, place, by_core, ties):
    shape = jax.ShapeDtypeStruct(ahead[0].shape, BF16)
    return pl.pallas_call(
        functools.partial(finish_body, len(ties), by_core),
        in_specs=[SMEM] + [VMEM] * 5 + [ANY] * len(ties),
        out_specs=[VMEM] * 2,
        out_shape=[shape] * 2,
        compiler_params=params(4),
        cost_estimate=QUICK,
        name="finish",
    )(place, partial, *ahead, *behind, *ties)


def gate_body(count, dims, place_ref, gain_ref, *refs):
    slots, chunks, parts = dims
    pieces = refs[:count]
    weights = refs[count : count + parts]
    down_ref, out_ref, away_ref, x_ref = refs[count + parts :]
    core = place_ref[1]
    half = x_ref.shape[2]
    tile = tile_of(out_ref.shape[1])
    steps = out_ref.shape[1] // tile

    low, high = gain_ref[:half].reshape(1, half), gain_ref[half:].reshape(1, half)
    own_gain = jnp.where(core == 0, low, high)
    got_gain = jnp.where(core == 0, high, low)
    at = iter(pieces)
    row = 0
    for _k in range(slots):
        owns = [next(at) for _c in range(chunks)]
        gots = [next(at) for _c in range(chunks)]
        for own, got in zip(owns, gots):
            own, got = own[...].astype(F32), got[...].astype(F32)
            n = own.shape[0]
            square = jnp.sum(own * own, axis=-1, keepdims=True) + jnp.sum(got * got, axis=-1, keepdims=True)
            scale = lax.rsqrt(square * (0.5 / half) + EPS)
            x_ref[core, row : row + n, :] = (own * scale * own_gain).astype(BF16)
            x_ref[1 - core, row : row + n, :] = (got * scale * got_gain).astype(BF16)
            row += n

    for j in range(steps):
        gate = up = None
        at = 0
        for p in range(parts):
            per = weights[p].shape[1]
            side, first = divmod(at, half)
            at += per
            x = x_ref[side, :, first : first + per]
            g = jnp.dot(x, weights[p][0, :, j * tile : (j + 1) * tile], preferred_element_type=F32)
            u = jnp.dot(x, weights[p][1, :, j * tile : (j + 1) * tile], preferred_element_type=F32)
            gate = g if gate is None else gate + g
            up = u if up is None else up + u
        out_ref[:, j * tile : (j + 1) * tile] = (gate / (1.0 + jnp.exp(-gate)) * up).astype(BF16)

    hidden = out_ref[...]
    wide = tile_of(half)
    for j in range(0, half, wide):
        away_ref[:, j : j + wide] = jnp.dot(hidden, down_ref[:, j : j + wide], preferred_element_type=F32).astype(BF16)


def gate_up(pieces, slots, chunks, weights, down, gain, place):
    half = gain.shape[0] // 2
    rows = slots * chunks * pieces[0].shape[0]
    parts = len(weights)
    units = weights[0].shape[2]
    return pl.pallas_call(
        functools.partial(gate_body, len(pieces), (slots, chunks, parts)),
        in_specs=[SMEM] + [VMEM] * (2 + len(pieces) + parts),
        out_specs=[VMEM] * 2,
        out_shape=[jax.ShapeDtypeStruct((rows, units), BF16), jax.ShapeDtypeStruct((rows, half), BF16)],
        scratch_shapes=[pltpu.VMEM((2, rows, half), BF16)],
        compiler_params=params(3 + rows * half * 18 // 2**20),
        cost_estimate=QUICK,
        name="gate_up",
    )(place, gain, *pieces, *weights, down)


def down_body(x_ref, w_ref, got_ref, out_ref):
    half = out_ref.shape[1]
    wide = tile_of(half)
    x = x_ref[...]
    for j in range(0, half, wide):
        out_ref[:, j : j + wide] = jnp.dot(x, w_ref[:, j : j + wide], preferred_element_type=F32)


def down_half(hidden, down):
    rows, units = hidden.shape
    half = down.shape[1]
    return pl.pallas_call(
        lambda x_ref, w_ref, out_ref: down_body(x_ref, w_ref, None, out_ref),
        in_specs=[VMEM] * 2,
        out_specs=VMEM,
        out_shape=jax.ShapeDtypeStruct((rows, half), F32),
        compiler_params=params(4 + rows * half * 4 // 2**20),
        cost_estimate=QUICK,
        name="down_half",
    )(hidden, down)


def make(mesh):
    n = mesh.shape["hid"]
    n_req = mesh.shape["req"]
    chips = n // 2
    both = [(h, h ^ 1) for h in range(n)]
    ring = [(h, (h + 2) % n) for h in range(n)]
    ring_back = [(h, (h - 2) % n) for h in range(n)]
    far = chips // 2

    def swap(v):
        return lax.ppermute(v, "hid", both)

    def onward(v):
        return lax.ppermute(v, "hid", ring)

    def back(v):
        return lax.ppermute(v, "hid", ring_back)

    def run(fillers, step, value):
        done = [f(value) for f in fillers[step]] if step < len(fillers) else []
        return [what for what, _ in done], [token for _, token in done]

    def rotate(own, fillers=()):
        slots = [list(own)]
        here = list(own)
        gave = []
        for k in range(1, chips):
            what, tokens = run(fillers, k - 1, here[-1])
            gave += what
            here = [onward(v) for v in here]
            if tokens:
                here = [pass_on(v, tokens) for v in here]
            slots.append(here)
        return [(s, [swap(v) for v in s]) for s in slots], gave

    def gather(own, fillers=()):
        slots = [None] * chips
        slots[0] = list(own)
        ahead, behind = list(own), list(own)
        gave = []
        for k in range(1, far + 1):
            what, tokens = run(fillers, k - 1, ahead[0])
            gave += what
            ahead[0], behind[1] = onward(ahead[0]), back(behind[1])
            if k < far:
                ahead[1], behind[0] = onward(ahead[1]), back(behind[0])
                ahead[0] = pass_on(ahead[0], [*tokens, ahead[1]])
                behind[1] = pass_on(behind[1], [*tokens, behind[0]])
                slots[k], slots[chips - k] = list(ahead), list(behind)
            else:
                if tokens:
                    ahead[0], behind[1] = pass_on(ahead[0], tokens), pass_on(behind[1], tokens)
                slots[far] = [ahead[0], behind[1]]
        return [(s, [swap(v) for v in s]) for s in slots], gave

    def scatter(partial, place, by_core, fillers=()):
        step = partial.shape[0] // (2 * chips)
        row = lambda slot, i: (2 * (slot % chips) + i) * step
        first = lambda slot, i: partial[row(slot, i) : row(slot, i) + step].astype(BF16)
        ahead = [first(far, 0), first(chips - far + 1, 1)]
        behind = [first(far - 1, 0), first(far, 1)]
        gave = []
        for d in range(far - 1, -1, -1):
            what, ties = run(fillers, far - 1 - d, ahead[0])
            gave += what
            ahead[0], behind[1] = onward(ahead[0]), back(behind[1])
            if d:
                ahead[1], behind[0] = onward(ahead[1]), back(behind[0])
                ahead[0] = add_slot(ahead[0], partial, row(chips - d, 0), [*ties, ahead[1]])
                behind[1] = add_slot(behind[1], partial, row(d, 1), [*ties, behind[0]])
            if d > 1:
                ahead[1] = add_slot(ahead[1], partial, row(chips - d + 1, 1), ties)
                behind[0] = add_slot(behind[0], partial, row(d - 1, 0), ties)
        return finish(ahead, behind, partial, place, by_core, ties), gave

    def per_device(tokens, gain_in, w_qkv, adapt_down, adapt_up, w_out, gain_ff, w_gate_up, w_down,
                   prefix_cache, prefix_owner, group_prefix, lengths):
        tok_dev, width_in = tokens.shape
        cols = w_qkv.shape[2]
        model_width = w_out.shape[1]
        half = model_width // 2
        hid = lax.axis_index("hid")
        req = lax.axis_index("req")
        core = hid % 2
        chip = hid // 2
        place = jnp.stack([chip, core, req]).astype(jnp.int32)

        here = norm_rows(tokens, gain_in[None, :], 2)
        w_t = jnp.transpose(w_qkv, (1, 2, 0)).reshape(3 * cols, width_in)

        def hold_weights(v):
            *held, token = hold(w_t, adapt_down, place, v)
            return held, token

        def split_out(v):
            *sides, token = halves(w_out, place, v)
            return sides, token

        def cached(v):
            mine, other = split_heads(candidates, place, prefix_owner, group_prefix, chips, [v])
            blocks = pack_blocks(mine, swap(other), place)
            return blocks, blocks[0]

        cache = prefix_cache[0]
        candidates = [cache] + [
            lax.ppermute(cache, "req", [(r, r ^ k) for r in range(n_req)]) for k in range(1, n_req)
        ]
        parts, first = [], 0
        for side in range(2):
            long = (half // 2 + 255) // 256 * 256
            for rows in (long, half - long):
                parts.append(lambda v, first=first, rows=rows: unpair(w_gate_up, first, rows, v))
                first += rows
        parts += [lambda v, flip=flip: bring(w_down, place, flip, v) for flip in (True, False)]

        slots, given = rotate(here, [[hold_weights], [split_out] + parts[:EARLY], [cached]])
        (w_t, adapt_down), (w_own, w_away), *early, kv_blocks = given
        kv_blocks = [
            lax.ppermute(block, "hid", [(h, h ^ (2 * k)) for h in range(n)]) if k else block
            for k, block in enumerate(kv_blocks)
        ]
        w_got = swap(w_away)

        pick = lambda i: [v for s in slots for v in (s[0][i], s[1][i])]
        acc, lat = project(pick(0), w_t, adapt_down, kv_blocks[1:])
        heads = attend(pick(1), w_t, adapt_down, adapt_up.T, kv_blocks, acc, lat, place, lengths, chips)
        partial = out_project(heads, swap(heads), w_own, w_got)

        late = parts[EARLY:]
        cuts = [0, *CUTS]
        late = [late[i:j] for i, j in zip(cuts, cuts[1:] + [len(late)])]
        sums, more = scatter(partial, place, False, late[:2])
        summed, rest = gather(sums, late[2:])
        *w_pairs, down_away, down_own = early + more + rest

        def first_output(_):
            attn_own = join(core_rows(summed[0][0], place), core_rows(summed[0][1], place), place)
            return attn_own, attn_own

        pieces = [v for s in summed for v in s[0] + s[1]]
        hidden, away_half = gate_up(pieces, chips, 2, w_pairs, down_away, gain_ff, place)
        got_half = swap(away_half)
        own_half = down_half(hidden, down_own)
        ends, (attn_own,) = scatter(own_half + got_half.astype(F32), place, True, [[first_output]])
        block_own = join(ends[0], swap(ends[1]), place)
        return attn_own, block_own

    return per_device


def solution(mesh):
    placed = (
        P(("req", "hid"), None),
        P(),
        P(None, None, "hid"),
        P(),
        P(None, "hid"),
        P("hid", None),
        P(),
        P(None, None, "hid"),
        P("hid", None),
        P("req", "hid", None, None),
        P(),
        P(),
        P("req", None),
    )
    return jax.shard_map(
        make(mesh),
        mesh=mesh,
        in_specs=placed,
        out_specs=(P(("req", "hid"), None), P(("req", "hid"), None)),
        check_vma=False,
    )
```

```python
import functools

import jax
import jax.numpy as jnp
from jax import lax
from jax.experimental import pallas as pl
from jax.experimental.pallas import tpu as pltpu
from jax.sharding import PartitionSpec as P

HD = 224
EPS = 1e-05
EARLY, EARLY_2 = 1, 1
CUTS = (1, 2, 4)
F32 = jnp.float32
BF16 = jnp.bfloat16
NT = (((1,), (1,)), ((), ()))
TN = (((0,), (0,)), ((), ()))
VMEM = pl.BlockSpec(memory_space=pltpu.VMEM)
SMEM = pl.BlockSpec(memory_space=pltpu.SMEM)
ANY = pl.BlockSpec(memory_space=pl.ANY)
TOKEN = jax.ShapeDtypeStruct((8, 128), F32)
QUICK = pl.CostEstimate(flops=1, bytes_accessed=1, transcendentals=0)
HBM = pl.BlockSpec(memory_space=pltpu.HBM)


def params(mib=56):
    return pltpu.CompilerParams(vmem_limit_bytes=mib * 2**20)


def split_cols(block, count):
    width = block.shape[1] // count
    return [block[:, i * width : (i + 1) * width] for i in range(count)]


def tile_of(width):
    return 256 if width % 256 == 0 else width


def norm_body(tok_ref, gain_ref, *refs):
    *outs, tok, gain, sems = refs
    copies = [
        pltpu.make_async_copy(tok_ref, tok, sems.at[0]),
        pltpu.make_async_copy(gain_ref, gain, sems.at[1]),
    ]
    for c in copies:
        c.start()
    for c in copies:
        c.wait()
    t = tok[...].astype(F32)
    scale = lax.rsqrt(jnp.mean(t * t, axis=-1, keepdims=True) + EPS)
    normed = (t * scale * gain[...]).astype(BF16)
    width = t.shape[1] // len(outs)
    for i, out in enumerate(outs):
        out[...] = normed[:, i * width : (i + 1) * width]


def norm_rows(tokens, gain, count):
    rows, width = tokens.shape
    return pl.pallas_call(
        norm_body,
        in_specs=[HBM, HBM],
        out_specs=[VMEM] * count,
        out_shape=[jax.ShapeDtypeStruct((rows, width // count), BF16)] * count,
        scratch_shapes=[
            pltpu.VMEM((rows, width), BF16),
            pltpu.VMEM((1, width), F32),
            pltpu.SemaphoreType.DMA((2,)),
        ],
        compiler_params=params(8),
        cost_estimate=QUICK,
        name="norm_rows",
    )(pltpu.with_memory_space_constraint(tokens, pltpu.HBM), pltpu.with_memory_space_constraint(gain, pltpu.HBM))


def unpair_body(first, w_ref, _, out_ref, token_ref, buf, sems):
    token_ref[...] = jnp.zeros_like(token_ref)
    count, step = buf.shape[:2]

    def fetch(i):
        return pltpu.make_async_copy(w_ref.at[pl.ds(first + i * step, step)], buf.at[i], sems.at[i])

    for i in range(count):
        fetch(i).start()
    for i in range(count):
        fetch(i).wait()
        out_ref[:, i * step : (i + 1) * step, :] = jnp.swapaxes(buf[i], 0, 1)


def unpair(weights, first, rows, after):
    _, two, width = weights.shape
    count = 4
    step = rows // count
    return pl.pallas_call(
        functools.partial(unpair_body, first),
        in_specs=[HBM, ANY],
        out_specs=[VMEM] * 2,
        out_shape=[jax.ShapeDtypeStruct((two, rows, width), BF16), TOKEN],
        scratch_shapes=[pltpu.VMEM((count, step, two, width), BF16), pltpu.SemaphoreType.DMA((count,))],
        compiler_params=params(11),
        cost_estimate=QUICK,
        name="unpair",
    )(pltpu.with_memory_space_constraint(weights, pltpu.HBM), after)


def hold_body(place_ref, w_ref, down_ref, _, w_out, down_out, token_ref, sems):
    token_ref[...] = jnp.zeros_like(token_ref)
    copies = [pltpu.make_async_copy(down_ref, down_out, sems.at[0])]
    count = sems.shape[0] - 1
    step = w_ref.shape[0] // count
    for i in range(count):
        rows = pl.ds(i * step, step)
        copies.append(pltpu.make_async_copy(w_ref.at[rows], w_out.at[rows], sems.at[1 + i]))
    for c in copies:
        c.start()
    for c in copies:
        c.wait()


def hold(w_t, down, place, after):
    return pl.pallas_call(
        hold_body,
        in_specs=[SMEM, HBM, HBM, ANY],
        out_specs=[VMEM] * 3,
        out_shape=[jax.ShapeDtypeStruct(w_t.shape, BF16), jax.ShapeDtypeStruct(down.shape, BF16), TOKEN],
        scratch_shapes=[pltpu.SemaphoreType.DMA((7,))],
        compiler_params=params(2),
        cost_estimate=QUICK,
        name="hold",
    )(place, pltpu.with_memory_space_constraint(w_t, pltpu.HBM), pltpu.with_memory_space_constraint(down, pltpu.HBM), after)


def bring_body(flip, place_ref, w_ref, _, out_ref, token_ref, sems):
    token_ref[...] = jnp.zeros_like(token_ref)
    units, half = out_ref.shape
    core = place_ref[1]
    at = pl.multiple_of((1 - core if flip else core) * half, 128)
    count = sems.shape[0]
    step = units // count

    def fetch(i):
        rows = pl.ds(i * step, step)
        return pltpu.make_async_copy(w_ref.at[rows, pl.ds(at, half)], out_ref.at[rows], sems.at[i])

    for i in range(count):
        fetch(i).start()
    for i in range(count):
        fetch(i).wait()


def bring(w_down, place, flip, after):
    units, width = w_down.shape
    return pl.pallas_call(
        functools.partial(bring_body, flip),
        in_specs=[SMEM, HBM, ANY],
        out_specs=[VMEM] * 2,
        out_shape=[jax.ShapeDtypeStruct((units, width // 2), BF16), TOKEN],
        scratch_shapes=[pltpu.SemaphoreType.DMA((8,))],
        compiler_params=params(2),
        cost_estimate=QUICK,
        name="bring",
    )(place, pltpu.with_memory_space_constraint(w_down, pltpu.HBM), after)


def stack_body(*refs):
    out_ref = refs[-1]
    for i, ref in enumerate(refs[:-1]):
        out_ref[i] = ref[...]


def stack(values):
    return pl.pallas_call(
        stack_body,
        in_specs=[VMEM] * len(values),
        out_specs=VMEM,
        out_shape=jax.ShapeDtypeStruct((len(values), *values[0].shape), BF16),
        compiler_params=params(4),
        cost_estimate=QUICK,
        name="stack",
    )(*values)


def pass_body(*_refs):
    pass


def pass_on(value, tokens):
    return pl.pallas_call(
        pass_body,
        in_specs=[ANY] * (1 + len(tokens)),
        out_specs=ANY,
        out_shape=jax.ShapeDtypeStruct(value.shape, value.dtype),
        input_output_aliases={0: 0},
        compiler_params=params(1),
        cost_estimate=QUICK,
        name="pass_on",
    )(value, *tokens)


def split_body(count, place_ref, owner_ref, group_ref, *refs):
    candidates = refs[:count]
    mine_ref, other_ref = refs[-2:]
    core, req = place_ref[1], place_ref[2]
    away = owner_ref[group_ref[req]] ^ req
    chips, two, cols, _ = mine_ref.shape
    chosen = candidates[0][...]
    for k in range(1, count):
        chosen = jnp.where(away == k, candidates[k][...], chosen)
    chosen = jnp.swapaxes(chosen, 0, 1).astype(F32)
    for kind in range(two):
        turned = chosen[kind].T.astype(BF16)
        for c in range(chips):
            even = turned[2 * c * cols : (2 * c + 1) * cols]
            odd = turned[(2 * c + 1) * cols : (2 * c + 2) * cols]
            mine_ref[c, kind] = jnp.where(core == 0, even, odd)
            other_ref[c, kind] = jnp.where(core == 0, odd, even)


def split_heads(candidates, place, owner, group, chips, ties):
    positions, two, width = candidates[0].shape
    shape = jax.ShapeDtypeStruct((chips, two, width // (2 * chips), positions), BF16)
    return pl.pallas_call(
        functools.partial(split_body, len(candidates)),
        in_specs=[SMEM] * 3 + [VMEM] * len(candidates) + [ANY] * len(ties),
        out_specs=[VMEM] * 2,
        out_shape=[shape] * 2,
        compiler_params=params(2 + candidates[0].size * 24 // 2**20),
        cost_estimate=QUICK,
        name="split_heads",
    )(place, owner, group, *candidates, *ties)


def pack_body(place_ref, mine_ref, got_ref, *outs):
    chip = place_ref[0]
    for k, out in enumerate(outs):
        for kind in range(out.shape[0]):
            out[kind] = jnp.concatenate([mine_ref[chip ^ k, kind], got_ref[chip ^ k, kind]], axis=1)


def pack_blocks(mine, got, place):
    chips = mine.shape[0]
    shape = jax.ShapeDtypeStruct((*mine.shape[1:3], 2 * mine.shape[3]), BF16)
    return pl.pallas_call(
        pack_body,
        in_specs=[SMEM, VMEM, VMEM],
        out_specs=[VMEM] * chips,
        out_shape=[shape] * chips,
        compiler_params=params(4),
        cost_estimate=QUICK,
        name="pack_blocks",
    )(place, mine, got)


def halves_body(place_ref, w_ref, _, own_ref, away_ref, token_ref, sems):
    token_ref[...] = jnp.zeros_like(token_ref)
    half = own_ref.shape[1]
    core = place_ref[1]
    copies = [
        pltpu.make_async_copy(w_ref.at[:, pl.ds(pl.multiple_of(side * half, 128), half)], out, sems.at[i])
        for i, (side, out) in enumerate(((core, own_ref), (1 - core, away_ref)))
    ]
    for c in copies:
        c.start()
    for c in copies:
        c.wait()


def halves(weights, place, after):
    rows, width = weights.shape
    shape = jax.ShapeDtypeStruct((rows, width // 2), BF16)
    return pl.pallas_call(
        halves_body,
        in_specs=[SMEM, HBM, ANY],
        out_specs=[VMEM] * 3,
        out_shape=[shape] * 2 + [TOKEN],
        scratch_shapes=[pltpu.SemaphoreType.DMA((2,))],
        compiler_params=params(2),
        cost_estimate=QUICK,
        name="halves",
    )(place, pltpu.with_memory_space_constraint(weights, pltpu.HBM), after)


def rows_body(count, place_ref, *refs):
    core = place_ref[1]
    out = refs[-1]
    step = refs[0].shape[0]
    for i in range(count // 2):
        out[i * step : (i + 1) * step, :] = jnp.where(core == 0, refs[i][...], refs[count // 2 + i][...])


def core_rows(chunks, place):
    step, width = chunks[0].shape
    count = len(chunks)
    return pl.pallas_call(
        functools.partial(rows_body, count),
        in_specs=[SMEM] + [VMEM] * count,
        out_specs=VMEM,
        out_shape=jax.ShapeDtypeStruct((step * count // 2, width), BF16),
        compiler_params=params(4),
        cost_estimate=QUICK,
        name="core_rows",
    )(place, *chunks)


def join_body(place_ref, near_ref, far_ref, out_ref):
    half = near_ref.shape[1]
    own = place_ref[1] == 0
    near, far = near_ref[...], far_ref[...]
    out_ref[:, :half] = jnp.where(own, near, far)
    out_ref[:, half:] = jnp.where(own, far, near)


def join(near, far, place):
    rows, half = near.shape
    return pl.pallas_call(
        join_body,
        in_specs=[SMEM, VMEM, VMEM],
        out_specs=VMEM,
        out_shape=jax.ShapeDtypeStruct((rows, 2 * half), BF16),
        compiler_params=params(4),
        cost_estimate=QUICK,
        name="join",
    )(place, near, far)


def project_part(pieces, part, w_ref, down_ref, rows_ref, acc_ref, lat_ref, acc, lat):
    at = 0
    for piece in pieces:
        n = piece.shape[-2]
        rows_ref[at : at + n, :] = piece[part] if len(piece.shape) == 3 else piece[...]
        at += n
    width = rows_ref.shape[1]
    kb = width // 4
    for s in range(4):
        x = rows_ref[:, s * kb : (s + 1) * kb]
        k = part * width + s * kb
        more = lax.dot_general(w_ref[:, k : k + kb], x, NT, preferred_element_type=F32)
        extra = jnp.dot(x, down_ref[k : k + kb, :], preferred_element_type=F32)
        if s == 0 and acc is None:
            acc_ref[...] = more
            lat_ref[...] = extra
        elif s == 0:
            acc_ref[...] = acc[...] + more
            lat_ref[...] = lat[...] + extra
        else:
            acc_ref[...] += more
            lat_ref[...] += extra


def project_body(count, ties, *refs):
    pieces = refs[:count]
    w_ref, down_ref, acc_ref, lat_ref, rows_ref = refs[count : count + 2] + refs[count + 2 + ties :]
    project_part(pieces, 0, w_ref, down_ref, rows_ref, acc_ref, lat_ref, None, None)


def attend_body(count, blocks, dims, place_ref, len_ref, *refs):
    pieces = refs[:count]
    kv_refs = refs[count : count + blocks]
    w_ref, down_ref, up_ref, acc_in, lat_in, out_ref, rows_ref, acc_ref, lat_ref = refs[count + blocks :]
    rows, cols, chips, tok_dev = dims
    project_part(pieces, 1, w_ref, down_ref, rows_ref, acc_ref, lat_ref, acc_in, lat_in)

    chip, core = place_ref[0], place_ref[1]
    keys_t = acc_ref[cols : 2 * cols, :].astype(BF16)
    vals_t = acc_ref[2 * cols :, :].astype(BF16)
    cached_k = jnp.concatenate([kv[0] for kv in kv_refs], axis=1)
    cached_v = jnp.concatenate([kv[1] for kv in kv_refs], axis=1)
    up = up_ref[...]
    scale = HD ** (-0.5)
    pair = 2 * tok_dev

    def spots(row):
        slot = row // pair
        inside = row - slot * pair
        side = inside // tok_dev
        owner = chip - slot
        owner = jnp.where(owner < 0, owner + chips, owner)
        at = jnp.where(core == 0, side, 1 - side)
        return owner * pair + at * tok_dev + inside - side * tok_dev

    def requests(spot):
        end = len_ref[0, 0]
        found = (spot >= end).astype(jnp.int32)
        for j in range(1, len_ref.shape[1]):
            end = end + len_ref[0, j]
            found = found + (spot >= end).astype(jnp.int32)
        return found

    block = min(256, rows)
    key_spot = spots(lax.broadcasted_iota(jnp.int32, (rows, 1), 0))
    key_req = requests(key_spot)

    def one_block(b, carry):
        r0 = pl.multiple_of(b * block, block)
        lat = lat_ref[pl.ds(r0, block), :].astype(BF16)
        q = acc_ref[:cols, pl.ds(r0, block)] + lax.dot_general(up, lat, NT, preferred_element_type=F32)
        q = q.astype(BF16)
        q_spot = spots(r0 + lax.broadcasted_iota(jnp.int32, (1, block), 1))
        allowed = jnp.logical_and(requests(q_spot) == key_req, key_spot <= q_spot)
        pre = lax.dot_general(cached_k, q, TN, preferred_element_type=F32) * scale
        suf = lax.dot_general(keys_t, q, TN, preferred_element_type=F32) * scale
        suf = jnp.where(allowed, suf, -jnp.inf)
        top = jnp.maximum(jnp.max(pre, axis=0, keepdims=True), jnp.max(suf, axis=0, keepdims=True))
        pre = jnp.exp(pre - top)
        suf = jnp.exp(suf - top)
        total = jnp.sum(pre, axis=0, keepdims=True) + jnp.sum(suf, axis=0, keepdims=True)
        weighted = jnp.dot(cached_v, pre.astype(BF16), preferred_element_type=F32) + jnp.dot(
            vals_t, suf.astype(BF16), preferred_element_type=F32
        )
        heads = (weighted / total).T.astype(BF16)
        for k in range(block // tok_dev):
            base = r0 + (k // 2) * pair
            shift = (core if k % 2 == 0 else 1 - core) * tok_dev
            at = pl.multiple_of(base + shift, tok_dev)
            out_ref[pl.ds(at, tok_dev), :] = heads[k * tok_dev : (k + 1) * tok_dev]
        return carry

    if rows == block:
        one_block(0, 0)
    else:
        lax.fori_loop(0, rows // block, one_block, 0)


def project(pieces, w_t, down, ties):
    rows = sum(p.shape[-2] for p in pieces)
    width = pieces[0].shape[1]
    cols3, rank = w_t.shape[0], down.shape[1]
    return pl.pallas_call(
        functools.partial(project_body, len(pieces), len(ties)),
        in_specs=[VMEM] * (len(pieces) + 2) + [ANY] * len(ties),
        out_specs=[VMEM] * 2,
        out_shape=[jax.ShapeDtypeStruct((cols3, rows), F32), jax.ShapeDtypeStruct((rows, rank), F32)],
        scratch_shapes=[pltpu.VMEM((rows, width), BF16)],
        compiler_params=params(6 + rows * width * 4 // 2**20),
        cost_estimate=QUICK,
        name="project",
    )(*pieces, w_t, down, *ties)


def attend(pieces, w_t, down, up_t, kv_blocks, acc, lat, place, lengths, chips):
    rows = sum(p.shape[-2] for p in pieces)
    width = pieces[0].shape[1]
    cols3, rank = w_t.shape[0], down.shape[1]
    cols = cols3 // 3
    dims = (rows, cols, chips, pieces[0].shape[0])
    return pl.pallas_call(
        functools.partial(attend_body, len(pieces), len(kv_blocks), dims),
        in_specs=[SMEM, SMEM] + [VMEM] * (len(pieces) + len(kv_blocks) + 5),
        out_specs=VMEM,
        out_shape=jax.ShapeDtypeStruct((rows, cols), BF16),
        scratch_shapes=[
            pltpu.VMEM((rows, width), BF16),
            pltpu.VMEM((cols3, rows), F32),
            pltpu.VMEM((rows, rank), F32),
        ],
        compiler_params=params(6 + rows * width * 5 // 2**20),
        cost_estimate=QUICK,
        name="attend",
    )(place, lengths, *pieces, *kv_blocks, w_t, down, up_t, acc, lat)


def out_body(a_ref, b_ref, wa_ref, wb_ref, out_ref):
    out_ref[...] = jnp.dot(a_ref[...], wa_ref[...], preferred_element_type=F32) + jnp.dot(
        b_ref[...], wb_ref[...], preferred_element_type=F32
    )


def out_project(own, got, w_own, w_got):
    rows, width = own.shape[0], w_own.shape[1]
    return pl.pallas_call(
        out_body,
        in_specs=[VMEM] * 4,
        out_specs=VMEM,
        out_shape=jax.ShapeDtypeStruct((rows, width), F32),
        compiler_params=params(4 + rows * width * 8 // 2**20),
        cost_estimate=QUICK,
        name="out_project",
    )(own, got, w_own, w_got)


def add_body(row, got_ref, part_ref, *rest):
    rows = got_ref.shape[0]
    out_ref = rest[-1]
    out_ref[...] = (got_ref[...].astype(F32) + part_ref[row : row + rows, :]).astype(BF16)


def add_slot(got, partial, row, ties=()):
    return pl.pallas_call(
        functools.partial(add_body, row),
        in_specs=[VMEM] * 2 + [ANY] * len(ties),
        out_specs=VMEM,
        out_shape=jax.ShapeDtypeStruct(got.shape, BF16),
        compiler_params=params(4),
        cost_estimate=QUICK,
        name="add_slot",
    )(got, partial, *ties)


def finish_body(ties, by_core, place_ref, part_ref, *refs):
    gots, outs = refs[:4], refs[4 + ties :]
    step = gots[0].shape[0]
    sums = []
    for i in range(2):
        total = part_ref[i * step : (i + 1) * step, :]
        total = total + gots[i][...].astype(F32) + gots[2 + i][...].astype(F32)
        sums.append(total.astype(BF16))
    if by_core:
        own = place_ref[1] == 0
        sums = [jnp.where(own, sums[0], sums[1]), jnp.where(own, sums[1], sums[0])]
    for out, value in zip(outs, sums):
        out[...] = value


def finish(ahead, behind, partial, place, by_core, ties):
    shape = jax.ShapeDtypeStruct(ahead[0].shape, BF16)
    return pl.pallas_call(
        functools.partial(finish_body, len(ties), by_core),
        in_specs=[SMEM] + [VMEM] * 5 + [ANY] * len(ties),
        out_specs=[VMEM] * 2,
        out_shape=[shape] * 2,
        compiler_params=params(4),
        cost_estimate=QUICK,
        name="finish",
    )(place, partial, *ahead, *behind, *ties)


def gate_body(count, dims, place_ref, gain_ref, *refs):
    slots, chunks, parts = dims
    pieces = refs[:count]
    weights = refs[count : count + parts]
    down_ref, out_ref, away_ref, x_ref = refs[count + parts :]
    core = place_ref[1]
    half = x_ref.shape[2]
    tile = tile_of(out_ref.shape[1])
    steps = out_ref.shape[1] // tile

    low, high = gain_ref[:half].reshape(1, half), gain_ref[half:].reshape(1, half)
    own_gain = jnp.where(core == 0, low, high)
    got_gain = jnp.where(core == 0, high, low)
    at = iter(pieces)
    row = 0
    for _k in range(slots):
        owns = [next(at) for _c in range(chunks)]
        gots = [next(at) for _c in range(chunks)]
        for own, got in zip(owns, gots):
            own, got = own[...].astype(F32), got[...].astype(F32)
            n = own.shape[0]
            square = jnp.sum(own * own, axis=-1, keepdims=True) + jnp.sum(got * got, axis=-1, keepdims=True)
            scale = lax.rsqrt(square * (0.5 / half) + EPS)
            x_ref[core, row : row + n, :] = (own * scale * own_gain).astype(BF16)
            x_ref[1 - core, row : row + n, :] = (got * scale * got_gain).astype(BF16)
            row += n

    for j in range(steps):
        gate = up = None
        at = 0
        for p in range(parts):
            per = weights[p].shape[1]
            side, first = divmod(at, half)
            at += per
            x = x_ref[side, :, first : first + per]
            g = jnp.dot(x, weights[p][0, :, j * tile : (j + 1) * tile], preferred_element_type=F32)
            u = jnp.dot(x, weights[p][1, :, j * tile : (j + 1) * tile], preferred_element_type=F32)
            gate = g if gate is None else gate + g
            up = u if up is None else up + u
        out_ref[:, j * tile : (j + 1) * tile] = (gate / (1.0 + jnp.exp(-gate)) * up).astype(BF16)

    hidden = out_ref[...]
    wide = tile_of(half)
    for j in range(0, half, wide):
        away_ref[:, j : j + wide] = jnp.dot(hidden, down_ref[:, j : j + wide], preferred_element_type=F32).astype(BF16)


def gate_up(pieces, slots, chunks, weights, down, gain, place):
    half = gain.shape[0] // 2
    rows = slots * chunks * pieces[0].shape[0]
    parts = len(weights)
    units = weights[0].shape[2]
    return pl.pallas_call(
        functools.partial(gate_body, len(pieces), (slots, chunks, parts)),
        in_specs=[SMEM] + [VMEM] * (2 + len(pieces) + parts),
        out_specs=[VMEM] * 2,
        out_shape=[jax.ShapeDtypeStruct((rows, units), BF16), jax.ShapeDtypeStruct((rows, half), BF16)],
        scratch_shapes=[pltpu.VMEM((2, rows, half), BF16)],
        compiler_params=params(3 + rows * half * 18 // 2**20),
        cost_estimate=QUICK,
        name="gate_up",
    )(place, gain, *pieces, *weights, down)


def down_body(x_ref, w_ref, got_ref, out_ref):
    half = out_ref.shape[1]
    wide = tile_of(half)
    x = x_ref[...]
    for j in range(0, half, wide):
        out_ref[:, j : j + wide] = jnp.dot(x, w_ref[:, j : j + wide], preferred_element_type=F32)


def down_half(hidden, down):
    rows, units = hidden.shape
    half = down.shape[1]
    return pl.pallas_call(
        lambda x_ref, w_ref, out_ref: down_body(x_ref, w_ref, None, out_ref),
        in_specs=[VMEM] * 2,
        out_specs=VMEM,
        out_shape=jax.ShapeDtypeStruct((rows, half), F32),
        compiler_params=params(4 + rows * half * 4 // 2**20),
        cost_estimate=QUICK,
        name="down_half",
    )(hidden, down)


def make(mesh):
    n = mesh.shape["hid"]
    n_req = mesh.shape["req"]
    chips = n // 2
    both = [(h, h ^ 1) for h in range(n)]
    ring = [(h, (h + 2) % n) for h in range(n)]
    ring_back = [(h, (h - 2) % n) for h in range(n)]
    far = chips // 2

    def swap(v):
        return lax.ppermute(v, "hid", both)

    def onward(v):
        return lax.ppermute(v, "hid", ring)

    def back(v):
        return lax.ppermute(v, "hid", ring_back)

    def run(fillers, step, value):
        done = [f(value) for f in fillers[step]] if step < len(fillers) else []
        tokens = [t for _, token in done for t in (token if isinstance(token, list) else [token])]
        return [what for what, _ in done], tokens

    def rotate(own, fillers=()):
        slots = [list(own)]
        here = list(own)
        gave = []
        for k in range(1, chips):
            what, tokens = run(fillers, k - 1, here[-1])
            gave += what
            if k == chips - 1:
                here = [stack(here)]
            here = [onward(v) for v in here]
            if tokens:
                here = [pass_on(v, tokens) for v in here]
            slots.append(here)
        return [(s, [swap(v) for v in s]) for s in slots], gave

    def gather(own, fillers=()):
        slots = [None] * chips
        slots[0] = list(own)
        ahead, behind = list(own), list(own)
        gave = []
        for k in range(1, far + 1):
            what, tokens = run(fillers, k - 1, ahead[0])
            gave += what
            ahead[0], behind[1] = onward(ahead[0]), back(behind[1])
            if k < far:
                ahead[1], behind[0] = onward(ahead[1]), back(behind[0])
                ahead[0] = pass_on(ahead[0], [*tokens, ahead[1]])
                behind[1] = pass_on(behind[1], [*tokens, behind[0]])
                slots[k], slots[chips - k] = list(ahead), list(behind)
            else:
                if tokens:
                    ahead[0], behind[1] = pass_on(ahead[0], tokens), pass_on(behind[1], tokens)
                slots[far] = [ahead[0], behind[1]]
        return [(s, [swap(v) for v in s]) for s in slots], gave

    def scatter(partial, place, by_core, fillers=()):
        step = partial.shape[0] // (2 * chips)
        row = lambda slot, i: (2 * (slot % chips) + i) * step
        first = lambda slot, i: partial[row(slot, i) : row(slot, i) + step].astype(BF16)
        ahead = [first(far, 0), first(chips - far + 1, 1)]
        behind = [first(far - 1, 0), first(far, 1)]
        gave = []
        for d in range(far - 1, -1, -1):
            what, ties = run(fillers, far - 1 - d, ahead[0])
            gave += what
            ahead[0], behind[1] = onward(ahead[0]), back(behind[1])
            if d:
                ahead[1], behind[0] = onward(ahead[1]), back(behind[0])
                ahead[0] = add_slot(ahead[0], partial, row(chips - d, 0), [*ties, ahead[1]])
                behind[1] = add_slot(behind[1], partial, row(d, 1), [*ties, behind[0]])
            if d > 1:
                ahead[1] = add_slot(ahead[1], partial, row(chips - d + 1, 1), ties)
                behind[0] = add_slot(behind[0], partial, row(d - 1, 0), ties)
        return finish(ahead, behind, partial, place, by_core, ties), gave

    def per_device(tokens, gain_in, w_qkv, adapt_down, adapt_up, w_out, gain_ff, w_gate_up, w_down,
                   prefix_cache, prefix_owner, group_prefix, lengths):
        tok_dev, width_in = tokens.shape
        cols = w_qkv.shape[2]
        model_width = w_out.shape[1]
        half = model_width // 2
        hid = lax.axis_index("hid")
        req = lax.axis_index("req")
        core = hid % 2
        chip = hid // 2
        place = jnp.stack([chip, core, req]).astype(jnp.int32)

        here = norm_rows(tokens, gain_in[None, :], 2)
        w_t = jnp.transpose(w_qkv, (1, 2, 0)).reshape(3 * cols, width_in)

        def hold_weights(v):
            *held, token = hold(w_t, adapt_down, place, v)
            return held, token

        def split_out(v):
            *sides, token = halves(w_out, place, v)
            return sides, token

        def cached(v):
            mine, other = split_heads(candidates, place, prefix_owner, group_prefix, chips, [v])
            blocks = pack_blocks(mine, swap(other), place)
            got = [
                lax.ppermute(block, "hid", [(h, h ^ (2 * k)) for h in range(n)])
                for k, block in enumerate(blocks)
                if k
            ]
            return [blocks[0], *got], got

        cache = prefix_cache[0]
        candidates = [cache] + [
            lax.ppermute(cache, "req", [(r, r ^ k) for r in range(n_req)]) for k in range(1, n_req)
        ]
        parts, first = [], 0
        for side in range(2):
            long = (half // 2 + 255) // 256 * 256
            for rows in (long, half - long):
                parts.append(lambda v, first=first, rows=rows: unpair(w_gate_up, first, rows, v))
                first += rows
        parts += [lambda v, flip=flip: bring(w_down, place, flip, v) for flip in (True, False)]

        slots, given = rotate(here, [[hold_weights], [split_out] + parts[:EARLY], parts[EARLY:EARLY_2] + [cached]])
        (w_t, adapt_down), (w_own, w_away), *early, kv_blocks = given
        w_got = swap(w_away)

        pick = lambda i: [v for near, far_side in slots for v in (near[min(i, len(near) - 1)], far_side[min(i, len(far_side) - 1)])]
        acc, lat = project(pick(0), w_t, adapt_down, ())
        heads = attend(pick(1), w_t, adapt_down, adapt_up.T, kv_blocks, acc, lat, place, lengths, chips)
        partial = out_project(heads, swap(heads), w_own, w_got)

        late = parts[EARLY_2:]
        cuts = [0, *CUTS]
        late = [late[i:j] for i, j in zip(cuts, cuts[1:] + [len(late)])]
        sums, more = scatter(partial, place, False, late[:2])
        summed, rest = gather(sums, late[2:])
        *w_pairs, down_away, down_own = early + more + rest

        def first_output(_):
            attn_own = join(core_rows(summed[0][0], place), core_rows(summed[0][1], place), place)
            return attn_own, attn_own

        pieces = [v for s in summed for v in s[0] + s[1]]
        hidden, away_half = gate_up(pieces, chips, 2, w_pairs, down_away, gain_ff, place)
        got_half = swap(away_half)
        own_half = down_half(hidden, down_own)
        ends, (attn_own,) = scatter(own_half + got_half.astype(F32), place, True, [[first_output]])
        block_own = join(ends[0], swap(ends[1]), place)
        return attn_own, block_own

    return per_device


def solution(mesh):
    placed = (
        P(("req", "hid"), None),
        P(),
        P(None, None, "hid"),
        P(),
        P(None, "hid"),
        P("hid", None),
        P(),
        P(None, None, "hid"),
        P("hid", None),
        P("req", "hid", None, None),
        P(),
        P(),
        P("req", None),
    )
    return jax.shard_map(
        make(mesh),
        mesh=mesh,
        in_specs=placed,
        out_specs=(P(("req", "hid"), None), P(("req", "hid"), None)),
        check_vma=False,
    )
```
